32 devices in a mesh: depth: 4 (over x, core), scan: 8 (over z, y).
Axes of the slice: x: 2, y: 2, z: 4, core: 2. Of those that a mesh axis runs over, the one named last changes fastest.
Arguments:
- transmission: float32 [4, 2, 512, 3072], P('depth', None, 'scan'), may hold values from -5 to 5
- probe: float32 [2, 256, 256], replicated, may hold values from -6 to 6
- exit_adjoint: float32 [2, 16, 2, 256, 256], P(None, 'scan'), may hold values from -6 to 6
- scan_row: int32 [2, 16], P(None, 'scan'), may hold values from 0 to 511, as said below
- scan_col: int32 [2, 16], P(None, 'scan'), may hold values from 0 to 2816
Outputs:
- object_grad: float32 [4, 2, 512, 3072], P('depth', None, 'scan')
- probe_grad: float32 [2, 256, 256], P(None, 'depth')
The draws below stay inside these ranges and needn't reach their ends.
Inputs may be any that keep to these rules, and one draw needn't show every extreme that they name: `scan_row`: entries 2 * j to 2 * (j + 1) - 1 of every batch lie in rows 64 * j to 64 * (j + 1) - 1: they are the positions of scan region j.
All inputs are finite; a program needn't handle non-finite values.
Results may differ from the reference program's by a relative error of at most 0.0075.
Values may be sent and summed in bfloat16 or wider, within the bound.
No kernel may reach another device: no remote copies, remote signals or barrier semaphores. Data moves between devices by JAX's collectives and lax.ppermute only.
A program may use at most 128 MiB of HBM per device.

```python
import math
import jax
import jax.numpy as jnp
from jax import lax

P_SIZE = 256
STRIP = 64
W = 3072
S_DEV = 1
NB = 2
POS_DEV = 2
NSL = 4
ROWS = 512
POSITIONS = 16


def draw_scan_row(key, part):
    key = jax.random.fold_in(key, 7)
    offset_key, first_key, last_key = jax.random.split(key, 3)
    offsets = jax.random.randint(offset_key, (NB, POSITIONS), 0, STRIP)
    regions = (jnp.arange(POSITIONS) // POS_DEV)[None, :]
    row_values = offsets + regions * STRIP
    first_pick = jax.random.randint(first_key, (), 0, POS_DEV)
    last_pick = jax.random.randint(last_key, (), 0, POS_DEV)
    row_values = row_values.at[0, first_pick].set(0)
    row_values = row_values.at[NB - 1, POSITIONS - POS_DEV + last_pick].set(ROWS - 1)
    return row_values.astype(jnp.int32)


def draw_scan_col(key, part):
    key = jax.random.fold_in(key, 13)
    value_key, low_key, high_key = jax.random.split(key, 3)
    col_values = jax.random.randint(value_key, (NB * POSITIONS,), 0, W - P_SIZE + 1)
    low_pick = jax.random.randint(low_key, (), 0, NB * POSITIONS // 2)
    high_pick = jax.random.randint(high_key, (), NB * POSITIONS // 2, NB * POSITIONS)
    col_values = col_values.at[low_pick].set(0)
    col_values = col_values.at[high_pick].set(W - P_SIZE)
    return col_values.reshape(NB, POSITIONS).astype(jnp.int32)


def block_scale(own_key, shape, cuts, low, largest):
    gain = 1.0
    for position, shards_of in cuts:
        draws = jax.random.uniform(jax.random.fold_in(jax.random.fold_in(own_key, 6), position), (shards_of,), jnp.float32, low / len(cuts), largest / len(cuts))
        gain = gain * jnp.repeat(jnp.exp(draws), shape[position] // shards_of).reshape((-1,) + (1,) * (len(shape) - 1 - position))
    return gain


def noise(key, shape, scale, reach, cuts=(), held_as=jnp.bfloat16):
    result = scale * jax.random.normal(key, shape, jnp.float32)
    if cuts:
        result = result * block_scale(key, shape, cuts, -0.22, 0.18)
    return jnp.clip(result, -reach, reach).astype(held_as)


def setup_inputs(seed: int = 0) -> dict:
    streams_of = jax.random.split(jax.random.key(seed), 6)
    transmission = noise(streams_of[0], (NSL, 2, ROWS, W), 0.7, 5.0, ((0, 4), (2, 8)), jnp.float32)
    probe = noise(streams_of[1], (2, P_SIZE, P_SIZE), 1.0, 6.0, (), jnp.float32)
    exit_adjoint = noise(streams_of[2], (NB, POSITIONS, 2, P_SIZE, P_SIZE), 1.0, 6.0, ((1, 8),), jnp.float32)
    scan_row = draw_scan_row(jax.random.fold_in(streams_of[5], 71), 0)
    scan_col = draw_scan_col(jax.random.fold_in(streams_of[5], 71), 0)
    return {"transmission": transmission, "probe": probe, "exit_adjoint": exit_adjoint, "scan_row": scan_row, "scan_col": scan_col}


fresnel = 0.25


def transfer(extent):
    indices = jnp.arange(extent)
    frequency = jnp.where(indices < extent // 2, indices, indices - extent).astype(jnp.float32)
    phases = (-math.pi * fresnel / extent) * frequency * frequency
    factor = lax.complex(jnp.cos(phases), jnp.sin(phases))
    return factor[:, None] * factor[None, :]


def propagate(fields, spectrum):
    return jnp.fft.ifft2(jnp.fft.fft2(fields) * spectrum)


def rounded(values):
    real_part = lax.optimization_barrier(jnp.real(values).astype(jnp.bfloat16)).astype(jnp.float32)
    imag_part = lax.optimization_barrier(jnp.imag(values).astype(jnp.bfloat16)).astype(jnp.float32)
    return lax.complex(real_part, imag_part)


def reference(transmission, probe, exit_adjoint, scan_row, scan_col):
    forward_kernel = transfer(P_SIZE)
    backward_kernel = jnp.conj(forward_kernel)
    extended = jnp.concatenate([transmission, transmission[:, :, :P_SIZE, :]], axis=2)
    probe_c = lax.complex(probe[0], probe[1])
    adjoints = lax.complex(exit_adjoint[:, :, 0], exit_adjoint[:, :, 1]).reshape(NB * POSITIONS, P_SIZE, P_SIZE)
    all_rows = scan_row.reshape(-1).astype(jnp.int32)
    all_cols = scan_col.reshape(-1).astype(jnp.int32)
    zero_index = jnp.zeros((), jnp.int32)

    def visit(carry_pair, inputs_now):
        gradient, probe_total = carry_pair
        row_start, col_start, adjoint_now = inputs_now
        anchor = (zero_index, zero_index, row_start, col_start)
        patch_block = lax.dynamic_slice(extended, anchor, (NSL, 2, P_SIZE, P_SIZE))
        patches = lax.complex(patch_block[:, 0], patch_block[:, 1])
        current = probe_c
        incident = []
        for layer in range(NSL):
            if layer > 0 and layer % S_DEV == 0:
                current = rounded(current)
            incident.append(current)
            current = propagate(patches[layer] * current, forward_kernel)
        updates = []
        current = adjoint_now
        for layer in reversed(range(NSL)):
            if layer + 1 < NSL and (layer + 1) % S_DEV == 0:
                current = rounded(current)
            spread_back = propagate(current, backward_kernel)
            updates.append(jnp.conj(incident[layer]) * spread_back)
            current = jnp.conj(patches[layer]) * spread_back
        update = jnp.stack(updates[::-1])
        update = jnp.stack([jnp.real(update), jnp.imag(update)], axis=1)
        before = lax.dynamic_slice(gradient, anchor, (NSL, 2, P_SIZE, P_SIZE))
        gradient = lax.dynamic_update_slice(gradient, before + update, anchor)
        return (gradient, probe_total + current), None

    start_grad = jnp.zeros((NSL, 2, ROWS + P_SIZE, W), jnp.float32)
    start_probe = lax.complex(jnp.zeros((P_SIZE, P_SIZE), jnp.float32), jnp.zeros((P_SIZE, P_SIZE), jnp.float32))
    (gradient, probe_total), _ = lax.scan(visit, (start_grad, start_probe), (all_rows, all_cols, adjoints))
    object_grad = gradient[:, :, :ROWS, :].at[:, :, :P_SIZE, :].add(gradient[:, :, ROWS:, :])
    probe_grad = jnp.stack([jnp.real(probe_total), jnp.imag(probe_total)])
    return object_grad, probe_grad
```

```python
import functools

import jax
import jax.numpy as jnp
import numpy as np
from jax import lax
from jax.experimental import pallas as pl
from jax.experimental.pallas import tpu as pltpu
from jax.sharding import PartitionSpec as P

fresnel = 0.25
LANES = 128
bf16 = jnp.bfloat16
f32 = jnp.float32


def propagator(extent):
    indices = np.arange(extent)
    frequency = np.where(indices < extent // 2, indices, indices - extent).astype(np.float64)
    factor = np.exp(-1j * np.pi * fresnel / extent * frequency * frequency)
    column = np.fft.ifft(factor)
    matrix = column[(indices[:, None] - indices[None, :]) % extent]
    return matrix.real, matrix.imag


def halves(matrix):
    high = matrix.astype(np.float32).astype(bf16)
    low = (matrix - high.astype(np.float64)).astype(np.float32).astype(bf16)
    return high, low


def tables(extent):
    real, imag = propagator(extent)
    left = halves(np.concatenate([real, imag], axis=0))
    right = halves(np.concatenate([real, imag], axis=1))
    left_table = np.concatenate([left[0], left[0], left[1]], axis=1)
    right_table = np.concatenate([right[0], right[0], right[1]], axis=0)
    return left_table, right_table


def split(values):
    high = values.astype(bf16)
    low = (values - high.astype(f32)).astype(bf16)
    return high, low


def propagate(fields, left, right):
    side = fields[0][0].shape[0]
    high, low = split(jnp.concatenate([part for field in fields for part in field], axis=1))
    middle = jnp.dot(left, jnp.concatenate([high, low, high], axis=0), preferred_element_type=f32)
    rows = []
    for index in range(len(fields)):
        by_real = middle[:side, 2 * index * side : 2 * (index + 1) * side]
        by_imag = middle[side:, 2 * index * side : 2 * (index + 1) * side]
        rows.append(by_real[:, :side] - by_imag[:, side:])
        rows.append(by_real[:, side:] + by_imag[:, :side])
    high, low = split(jnp.concatenate(rows, axis=0))
    result = jnp.dot(jnp.concatenate([high, low, high], axis=1), right, preferred_element_type=f32)
    results = []
    for index in range(len(fields)):
        real = result[2 * index * side : (2 * index + 1) * side]
        imag = result[(2 * index + 1) * side : 2 * (index + 1) * side]
        results.append((real[:, :side] - imag[:, side:], real[:, side:] + imag[:, :side]))
    return results


def multiply(first, second):
    return (
        first[0] * second[0] - first[1] * second[1],
        first[0] * second[1] + first[1] * second[0],
    )


def turned(values, down, across):
    return pltpu.roll(pltpu.roll(values, down, 0), across, 1)


def turned_back(values, down, across):
    rows, columns = values.shape
    return turned(values, lax.rem(rows - down, rows), lax.rem(columns - across, columns))


def stretch(column, side, width):
    base = pl.multiple_of(column // LANES * LANES, LANES)
    after = pl.multiple_of(jnp.minimum(base + side, width - LANES), LANES)
    return base, after, column - base


def this_place():
    section = lax.axis_index("depth")
    return section % 2, section // 2


def column_of(places, width, *index):
    return lax.rem(places[index], width)


def window_place(places, home, turn, strip, width, flip=0):
    core, _ = this_place()
    regions = lax.axis_size("scan")
    source = lax.rem(lax.axis_index("scan") - home + regions, regions)
    value = places[core ^ flip, turn]
    return value // width - source * strip, lax.rem(lax.rem(value, width), LANES)


def pick_kernel(waves, out, buffer, arrived):
    core, half = this_place()
    copy = pltpu.make_async_copy(waves.at[core, 1 - half], buffer, arrived)
    copy.start()
    copy.wait()
    out[...] = buffer[...].astype(bf16)


def extract_kernel(reach, *refs):
    places, (strip, *outs) = refs[:reach], refs[reach:]
    count, _, rows, side = outs[0].shape
    width = strip.shape[2]
    core, _ = this_place()
    lane = lax.broadcasted_iota(jnp.int32, (rows, LANES), 1)
    for flip in range(2):
        for step in range(reach):
            out = outs[flip * reach + step]
            for turn in range(count):
                column = column_of(places[step], width, core ^ flip, turn)
                base, after, begin = stretch(column, side, width)
                rest = pl.multiple_of(base + LANES, LANES)
                for plane in range(2):
                    first = strip[plane, :, pl.ds(base, LANES)]
                    again = strip[plane, :, pl.ds(after, LANES)]
                    out[turn, plane, :, :LANES] = jnp.where(lane < begin, again, first).astype(bf16)
                    out[turn, plane, :, LANES:] = strip[plane, :, pl.ds(rest, side - LANES)].astype(
                        bf16
                    )


def start_kernel(home, strip, width, places, probe, *refs):
    adjoints, (left, right, out) = refs[:-3], refs[-3:]
    _, half = this_place()

    @pl.when(half == 0)
    def _():
        for turn in range(len(adjoints)):
            down, across = window_place(places, home, turn, strip, width)
            for plane in range(2):
                out[turn, plane] = turned(probe[plane], down, across)

    @pl.when(half != 0)
    def _():
        fields = []
        for turn, adjoint in enumerate(adjoints):
            down, across = window_place(places, home, turn, strip, width)
            real, imag = (turned(adjoint[plane].astype(f32), down, across) for plane in range(2))
            fields.append((real, -imag))
        for turn, field in enumerate(propagate(fields, left[...], right[...])):
            out[turn, 0], out[turn, 1] = field


def pair(ref, *index):
    return ref[(*index, 0)].astype(f32), ref[(*index, 1)].astype(f32)


def own_first():
    core, half = this_place()
    return jnp.where(core == half, 0, 1)


def near_kernel(home, width, places, start, left, right, *refs):
    pieces, (frames, waves, sent) = refs[:-3], refs[-3:]
    reach = len(pieces) // 2
    count, _, strip, side = pieces[0].shape
    own = own_first()
    row = lax.broadcasted_iota(jnp.int32, (strip, side), 0)
    for flip in range(2):
        parts = pieces[flip * reach : (flip + 1) * reach]
        for turn in range(count):
            down, _ = window_place(places, home, turn, strip, width)
            for plane in range(2):
                first = parts[0][turn, plane].astype(f32)
                again = parts[-1][turn, plane].astype(f32)
                frames[own ^ flip, turn, plane, :strip] = jnp.where(
                    row < down, again, first
                ).astype(bf16)
                for step in range(1, reach - 1):
                    frames[own ^ flip, turn, plane, step * strip : (step + 1) * strip] = parts[step][
                        turn, plane
                    ]
    fields = [multiply(pair(frames, 0, turn), pair(start, turn)) for turn in range(count)]
    for turn, field in enumerate(propagate(fields, left[...], right[...])):
        waves[turn, 0], waves[turn, 1] = field
        real, imag = multiply(pair(frames, 1, turn), field)
        sent[turn, 0] = real.astype(bf16)
        sent[turn, 1] = imag.astype(bf16)


def far_kernel(start, left, right, frames, waves, arrived, kept, given, last):
    count = start.shape[0]
    own = own_first()
    fields = propagate([pair(arrived, turn) for turn in range(count)], left[...], right[...])
    outer, inner = [], []
    for turn, field in enumerate(fields):
        outer.append(multiply(pair(waves, turn), field))
        inner.append(multiply(pair(frames, 1, turn), field))
    for turn, field in enumerate(propagate(inner, left[...], right[...])):
        first = multiply(pair(start, turn), field)
        for plane, sign in ((0, 1.0), (1, -1.0)):
            mine = jnp.where(own == 0, first[plane], outer[turn][plane])
            other = jnp.where(own == 0, outer[turn][plane], first[plane])
            kept[turn, plane] = (mine * sign).astype(bf16)
            given[turn, plane] = (other * sign).astype(bf16)
        last[turn, 0], last[turn, 1] = multiply(pair(frames, 0, turn), field)


def part_kernel(home, width, places, kept, arrived, *outs):
    _, count, _, strip, side = outs[0].shape
    row = lax.broadcasted_iota(jnp.int32, (strip, side), 0)
    for flip, windows in enumerate((kept, arrived)):
        for turn in range(count):
            down, _ = window_place(places, home, turn, strip, width, flip)
            for plane in range(2):
                ends = windows[turn, plane, :strip].astype(f32)
                outs[0][flip, turn, plane] = jnp.where(row < down, 0.0, ends).astype(bf16)
                outs[-1][flip, turn, plane] = jnp.where(row < down, ends, 0.0).astype(bf16)
                for step in range(1, len(outs) - 1):
                    outs[step][flip, turn, plane] = windows[
                        turn, plane, step * strip : (step + 1) * strip
                    ]


def probe_kernel(home, strip, width, places, waves, near, away, sent, total):
    core, half = this_place()
    weight = jnp.where(half == 0, 1.0, 0.0)
    for plane, sign in ((0, weight), (1, -weight)):
        parts = []
        for turn in range(waves.shape[0]):
            down, across = window_place(places, home, turn, strip, width)
            parts.append(turned_back(waves[turn, plane], down, across))
        total[plane] = sum(parts) * sign
    height = near.shape[1]
    for index, out in enumerate((near, away)):
        for plane in range(2):
            mine = pl.multiple_of((2 * index + core) * height, height)
            other = pl.multiple_of((2 * index + (core ^ 1)) * height, height)
            out[plane] = total[plane, pl.ds(mine, height)]
            sent[index, plane] = total[plane, pl.ds(other, height)].astype(bf16)


def deposit_kernel(reach, *refs):
    places, pieces, (out, total, done) = refs[:reach], refs[reach : 2 * reach], refs[2 * reach :]
    _, count, _, strip, side = pieces[0].shape
    width = out.shape[2]
    core, _ = this_place()
    stretches = []
    for step in range(reach):
        for flip in range(2):
            for turn in range(count):
                column = column_of(places[step], width, core ^ flip, turn)
                stretches.append((pieces[step].at[flip, turn], *stretch(column, side, width)))
    height = strip // 4
    lane = lax.broadcasted_iota(jnp.int32, (height, LANES), 1)
    copies = []
    for plane in range(2):
        for start in range(0, strip, height):
            rows = pl.ds(start, height)
            total[plane, rows] = jnp.zeros((height, width), f32)
            for piece, base, after, begin in stretches:
                rest = pl.multiple_of(base + LANES, LANES)
                ends = piece[plane, rows, :LANES].astype(f32)
                total[plane, rows, pl.ds(base, LANES)] += jnp.where(lane < begin, 0.0, ends)
                total[plane, rows, pl.ds(rest, side - LANES)] += piece[plane, rows, LANES:].astype(
                    f32
                )
                total[plane, rows, pl.ds(after, LANES)] += jnp.where(lane < begin, ends, 0.0)
            copy = pltpu.make_async_copy(
                total.at[plane, rows], out.at[plane, rows], done.at[len(copies)]
            )
            copy.start()
            copies.append(copy)
    for copy in copies:
        copy.wait()


def local(transmission, probe, exit_adjoint, scan_row, scan_col):
    depth = lax.axis_size("depth")
    regions = lax.axis_size("scan")
    strip, width = transmission.shape[2:]
    side = probe.shape[1]
    reach = side // strip + 1
    home = reach // 2
    count = scan_row.shape[1]
    assert transmission.shape[0] == 1 and depth == 4 and scan_row.shape[0] == 2
    assert side == 2 * LANES and count == 2

    half = lax.axis_index("depth") // (depth // 2)
    once = lax.axis_index("depth") // depth + 1

    def along_scan(value, by):
        return lax.ppermute(value, "scan", [(i, (i + by) % regions) for i in range(regions)])

    def across(value, flip, by, sections=range(depth)):
        if flip == 0 and by == 0:
            return value
        route = [
            (d * regions + i, (d ^ flip) * regions + (i + by) % regions)
            for d in sections
            for i in range(regions)
        ]
        return lax.ppermute(value, ("depth", "scan"), route)

    smem = pl.BlockSpec(memory_space=pltpu.SMEM)
    vmem = pl.BlockSpec(memory_space=pltpu.VMEM)

    def call(kernel, out_shape, in_specs, flops, name, scratch=(), out_spec=vmem):
        return pl.pallas_call(
            kernel,
            out_shape=out_shape,
            in_specs=in_specs,
            out_specs=jax.tree.map(lambda _: out_spec, out_shape),
            scratch_shapes=scratch,
            compiler_params=pltpu.CompilerParams(vmem_limit_bytes=24 * 1024 * 1024),
            cost_estimate=pl.CostEstimate(flops=flops, bytes_accessed=4 << 20, transcendentals=0),
            name=name,
        )

    shape = jax.ShapeDtypeStruct
    piece = shape((count, 2, strip, side), bf16)
    wave = (2, side, side)
    field = (count,) + wave
    left, right = (jnp.asarray(table) for table in tables(side))
    lower = range(depth // 2)

    adjoint = call(
        pick_kernel,
        shape(wave, bf16),
        [pl.BlockSpec(memory_space=pltpu.HBM)],
        1 << 20,
        "pick",
        [pltpu.VMEM(wave, f32), pltpu.SemaphoreType.DMA],
    )(exit_adjoint)
    packed = scan_row * width + scan_col
    adjoint, packed = lax.optimization_barrier((adjoint, packed))
    adjoint = along_scan(adjoint, home)
    places = [packed] + [along_scan(packed, step) for step in range(1, reach)]

    order = [(flip, step) for flip in range(2) for step in range(reach)]
    far_first = sorted(order, key=lambda key: -abs(key[1] - home))
    pieces = call(
        functools.partial(extract_kernel, reach),
        [piece] * len(order),
        [smem] * reach + [vmem],
        1 << 26,
        "extract",
    )(*places, transmission[0])
    pieces = dict(zip(order, pieces))
    adjoint, pieces[0, home] = lax.optimization_barrier((adjoint, pieces[0, home]))
    flipped = lax.fori_loop(0, once, lambda _, held: across(held, 2, 0, lower), adjoint)
    adjoints = [adjoint, flipped]
    for flip, step in far_first:
        pieces[flip, step] = across(pieces[flip, step], flip, home - step)

    start = call(
        functools.partial(start_kernel, home, strip, width),
        shape(field, f32),
        [smem] + [vmem] * (3 + count),
        1 << 30,
        "start",
    )(places[home], probe, *adjoints, left, right)
    frames, waves, sent = call(
        functools.partial(near_kernel, home, width),
        [shape((2,) + field, bf16), shape(field, f32), shape(field, bf16)],
        [smem] + [vmem] * (3 + len(order)),
        1 << 31,
        "near",
    )(places[home], start, left, right, *(pieces[key] for key in order))
    arrived = across(sent, 2, 0)
    kept, given, last = call(
        far_kernel,
        [shape(field, bf16)] * 2 + [shape(field, f32)],
        [vmem] * 6,
        1 << 32,
        "far",
    )(start, left, right, frames, waves, arrived)
    parts = call(
        functools.partial(part_kernel, home, width),
        [shape((2,) + piece.shape, bf16)] * reach,
        [smem] + [vmem] * 2,
        1 << 26,
        "part",
    )(places[home], kept, across(given, 1, 0))
    parts = list(parts)

    height = side // depth
    near, away, probe_sent = call(
        functools.partial(probe_kernel, home, strip, width),
        [shape((2, height, side), f32)] * 2 + [shape((2, 2, height, side), bf16)],
        [smem, vmem],
        1 << 26,
        "probe",
        [pltpu.VMEM(wave, f32)],
    )(places[home], last)
    returned = [across(part, 0, step - home) for step, part in enumerate(parts)]

    def probe_rounds(_, held):
        near, away, given = held
        given = given.astype(f32)
        away = across((away + given[1]).astype(bf16), 2, 0, lower).astype(f32)
        total = jnp.where(half == 0, near + given[0], away)
        if regions & (regions - 1):
            total = lax.psum(total, "scan")
        else:
            span = 1
            while span < regions:
                rounded = total.astype(bf16)
                route = [(i, i ^ span) for i in range(regions)]
                total = rounded.astype(f32) + lax.ppermute(rounded, "scan", route).astype(f32)
                span *= 2
        return total, away, held[2]

    near, parts[home] = lax.optimization_barrier((near, parts[home]))
    probe_grad, *_ = lax.fori_loop(
        0, once, probe_rounds, (near, away, across(probe_sent, 1, 0))
    )
    probe_grad, returned[home] = lax.optimization_barrier((probe_grad, parts[home]))
    object_grad = call(
        functools.partial(deposit_kernel, reach),
        shape(transmission.shape[1:], f32),
        [smem] * reach + [vmem] * reach,
        1 << 26,
        "deposit",
        [pltpu.VMEM(transmission.shape[1:], f32), pltpu.SemaphoreType.DMA((8,))],
        pl.BlockSpec(memory_space=pltpu.HBM),
    )(*places, *returned)
    return object_grad[None], probe_grad


def solution(mesh):
    placed = (
        P("depth", None, "scan", None),
        P(),
        P(None, "scan", None, None, None),
        P(None, "scan"),
        P(None, "scan"),
    )
    return jax.shard_map(
        local,
        mesh=mesh,
        in_specs=placed,
        out_specs=(P("depth", None, "scan", None), P(None, "depth", None)),
        check_vma=False,
    )
```

```python
import functools

import jax
import jax.numpy as jnp
import numpy as np
from jax import lax
from jax.experimental import pallas as pl
from jax.experimental.pallas import tpu as pltpu
from jax.sharding import PartitionSpec as P

fresnel = 0.25
LANES = 128
bf16 = jnp.bfloat16
f32 = jnp.float32


def propagator(extent):
    indices = np.arange(extent)
    frequency = np.where(indices < extent // 2, indices, indices - extent).astype(np.float64)
    factor = np.exp(-1j * np.pi * fresnel / extent * frequency * frequency)
    column = np.fft.ifft(factor)
    matrix = column[(indices[:, None] - indices[None, :]) % extent]
    return matrix.real, matrix.imag


def halves(matrix):
    high = matrix.astype(np.float32).astype(bf16)
    low = (matrix - high.astype(np.float64)).astype(np.float32).astype(bf16)
    return high, low


def tables(extent):
    real, imag = propagator(extent)
    left = halves(np.concatenate([real, imag], axis=0))
    right = halves(np.concatenate([real, imag], axis=1))
    left_table = np.concatenate([left[0], left[0], left[1]], axis=1)
    right_table = np.concatenate([right[0], right[0], right[1]], axis=0)
    return left_table, right_table


def split(values):
    high = values.astype(bf16)
    low = (values - high.astype(f32)).astype(bf16)
    return high, low


def propagate(fields, left, right):
    side = fields[0][0].shape[0]

    def parts(values, axis):
        high, low = split(values)
        if left.shape[1] == 3 * side:
            return jnp.concatenate([high, low, high], axis=axis)
        return jnp.concatenate([high, high], axis=axis)

    columns = parts(jnp.concatenate([part for field in fields for part in field], axis=1), 0)
    middle = jnp.dot(left, columns, preferred_element_type=f32)
    rows = []
    for index in range(len(fields)):
        by_real = middle[:side, 2 * index * side : 2 * (index + 1) * side]
        by_imag = middle[side:, 2 * index * side : 2 * (index + 1) * side]
        rows.append(by_real[:, :side] - by_imag[:, side:])
        rows.append(by_real[:, side:] + by_imag[:, :side])
    result = jnp.dot(parts(jnp.concatenate(rows, axis=0), 1), right, preferred_element_type=f32)
    results = []
    for index in range(len(fields)):
        real = result[2 * index * side : (2 * index + 1) * side]
        imag = result[(2 * index + 1) * side : 2 * (index + 1) * side]
        results.append((real[:, :side] - imag[:, side:], real[:, side:] + imag[:, :side]))
    return results


def multiply(first, second):
    return (
        first[0] * second[0] - first[1] * second[1],
        first[0] * second[1] + first[1] * second[0],
    )


def turned(values, down, across):
    return pltpu.roll(pltpu.roll(values, down, 0), across, 1)


def turned_back(values, down, across):
    rows, columns = values.shape
    return turned(values, lax.rem(rows - down, rows), lax.rem(columns - across, columns))


def stretch(column, side, width):
    base = pl.multiple_of(column // LANES * LANES, LANES)
    after = pl.multiple_of(jnp.minimum(base + side, width - LANES), LANES)
    return base, after, column - base


def this_place():
    section = lax.axis_index("depth")
    return section % 2, section // 2


def column_of(places, width, *index):
    return lax.rem(places[index], width)


def window_place(places, home, turn, strip, width, flip=0):
    core, _ = this_place()
    regions = lax.axis_size("scan")
    source = lax.rem(lax.axis_index("scan") - home + regions, regions)
    value = places[core ^ flip, turn]
    return value // width - source * strip, lax.rem(lax.rem(value, width), LANES)


def pick_kernel(waves, out, buffer, arrived):
    core, half = this_place()
    copy = pltpu.make_async_copy(waves.at[core, 1 - half], buffer, arrived)
    copy.start()
    copy.wait()
    out[...] = buffer[...].astype(bf16)


def extract_kernel(reach, *refs):
    places, (strip, *outs) = refs[:reach], refs[reach:]
    count, _, rows, side = outs[0].shape
    width = strip.shape[2]
    core, _ = this_place()
    lane = lax.broadcasted_iota(jnp.int32, (rows, LANES), 1)
    for flip in range(2):
        for step in range(reach):
            out = outs[flip * reach + step]
            for turn in range(count):
                column = column_of(places[step], width, core ^ flip, turn)
                base, after, begin = stretch(column, side, width)
                rest = pl.multiple_of(base + LANES, LANES)
                for plane in range(2):
                    first = strip[plane, :, pl.ds(base, LANES)]
                    again = strip[plane, :, pl.ds(after, LANES)]
                    out[turn, plane, :, :LANES] = jnp.where(lane < begin, again, first).astype(bf16)
                    out[turn, plane, :, LANES:] = strip[plane, :, pl.ds(rest, side - LANES)].astype(
                        bf16
                    )


def start_kernel(home, strip, width, places, probe, *refs):
    adjoints, (left, right, out) = refs[:-3], refs[-3:]
    _, half = this_place()

    @pl.when(half == 0)
    def _():
        for turn in range(len(adjoints)):
            down, across = window_place(places, home, turn, strip, width)
            for plane in range(2):
                out[turn, plane] = turned(probe[plane], down, across)

    @pl.when(half != 0)
    def _():
        fields = []
        for turn, adjoint in enumerate(adjoints):
            down, across = window_place(places, home, turn, strip, width)
            real, imag = (turned(adjoint[plane].astype(f32), down, across) for plane in range(2))
            fields.append((real, -imag))
        for turn, field in enumerate(propagate(fields, left[...], right[...])):
            out[turn, 0], out[turn, 1] = field


def pair(ref, *index):
    return ref[(*index, 0)].astype(f32), ref[(*index, 1)].astype(f32)


def own_first():
    core, half = this_place()
    return jnp.where(core == half, 0, 1)


def near_kernel(home, turn, early, width, places, start, left, right, *refs):
    pieces, (frames, wave, sent) = refs[:-3], refs[-3:]
    reach = len(pieces) // 2
    _, _, strip, side = pieces[0].shape
    own = own_first()
    row = lax.broadcasted_iota(jnp.int32, (strip, side), 0)
    down, _ = window_place(places, home, turn, strip, width)
    for flip in range(2):
        parts = pieces[flip * reach : (flip + 1) * reach]
        for plane in range(2):
            first = parts[0][turn, plane].astype(f32)
            again = parts[-1][turn, plane].astype(f32)
            frames[own ^ flip, plane, :strip] = jnp.where(row < down, again, first).astype(bf16)
            for step in range(1, reach - 1):
                frames[own ^ flip, plane, step * strip : (step + 1) * strip] = parts[step][
                    turn, plane
                ]
    field = multiply(pair(frames, 0), pair(start, turn))
    if early:
        (field,) = propagate([field], left[:, side:], right[side:])
        wave[0], wave[1] = field
        real, imag = multiply(pair(frames, 1), field)
    else:
        (field,) = propagate([field], left[...], right[...])
        wave[0], wave[1] = field
        ((real, imag),) = propagate([multiply(pair(frames, 1), field)], left[...], right[...])
    sent[0] = real.astype(bf16)
    sent[1] = imag.astype(bf16)


def far_kernel(turn, early, start, left, right, frames, wave, arrived, kept, given, last):
    own = own_first()
    side = start.shape[2]
    field = pair(arrived)
    if early:
        (field,) = propagate([field], left[...], right[...])
        outer = multiply(pair(wave), field)
        (field,) = propagate([multiply(pair(frames, 1), field)], left[...], right[...])
    else:
        outer = multiply(pair(wave), field)
        (field,) = propagate([multiply(pair(frames, 1), field)], left[:, side:], right[side:])
    first = multiply(pair(start, turn), field)
    for plane, sign in ((0, 1.0), (1, -1.0)):
        kept[plane] = (jnp.where(own == 0, first[plane], outer[plane]) * sign).astype(bf16)
        given[plane] = (jnp.where(own == 0, outer[plane], first[plane]) * sign).astype(bf16)
    last[0], last[1] = multiply(pair(frames, 0), field)


def part_kernel(home, width, places, *refs):
    count = places.shape[1]
    windows, outs = refs[: 2 * count], refs[2 * count :]
    _, _, _, strip, side = outs[0].shape
    row = lax.broadcasted_iota(jnp.int32, (strip, side), 0)
    for flip in range(2):
        for turn in range(count):
            window = windows[flip * count + turn]
            down, _ = window_place(places, home, turn, strip, width, flip)
            for plane in range(2):
                ends = window[plane, :strip].astype(f32)
                outs[0][flip, turn, plane] = jnp.where(row < down, 0.0, ends).astype(bf16)
                outs[-1][flip, turn, plane] = jnp.where(row < down, ends, 0.0).astype(bf16)
                for step in range(1, len(outs) - 1):
                    outs[step][flip, turn, plane] = window[
                        plane, step * strip : (step + 1) * strip
                    ]


def probe_kernel(home, strip, width, places, *refs):
    waves, (near, away, sent, total) = refs[:-4], refs[-4:]
    core, half = this_place()
    weight = jnp.where(half == 0, 1.0, 0.0)
    for plane, sign in ((0, weight), (1, -weight)):
        parts = []
        for turn, wave in enumerate(waves):
            down, across = window_place(places, home, turn, strip, width)
            parts.append(turned_back(wave[plane], down, across))
        total[plane] = sum(parts) * sign
    height = near.shape[1]
    for index, out in enumerate((near, away)):
        for plane in range(2):
            mine = pl.multiple_of((2 * index + core) * height, height)
            other = pl.multiple_of((2 * index + (core ^ 1)) * height, height)
            out[plane] = total[plane, pl.ds(mine, height)]
            sent[index, plane] = total[plane, pl.ds(other, height)].astype(bf16)


def deposit_kernel(reach, *refs):
    places, pieces, out = refs[:reach], refs[reach:-1], refs[-1]
    _, count, _, strip, side = pieces[0].shape
    width = out.shape[2]
    core, _ = this_place()
    lane = lax.broadcasted_iota(jnp.int32, (strip, LANES), 1)
    out[...] = jnp.zeros(out.shape, f32)
    for step, piece in enumerate(pieces):
        for flip in range(2):
            for turn in range(count):
                column = column_of(places[step], width, core ^ flip, turn)
                base, after, begin = stretch(column, side, width)
                rest = pl.multiple_of(base + LANES, LANES)
                for plane in range(2):
                    ends = piece[flip, turn, plane, :, :LANES].astype(f32)
                    out[plane, :, pl.ds(base, LANES)] += jnp.where(lane < begin, 0.0, ends)
                    out[plane, :, pl.ds(rest, side - LANES)] += piece[
                        flip, turn, plane, :, LANES:
                    ].astype(f32)
                    out[plane, :, pl.ds(after, LANES)] += jnp.where(lane < begin, ends, 0.0)


def local(transmission, probe, exit_adjoint, scan_row, scan_col):
    depth = lax.axis_size("depth")
    regions = lax.axis_size("scan")
    strip, width = transmission.shape[2:]
    side = probe.shape[1]
    reach = side // strip + 1
    home = reach // 2
    count = scan_row.shape[1]
    assert transmission.shape[0] == 1 and depth == 4 and scan_row.shape[0] == 2
    assert side == 2 * LANES and count == 2

    def along_scan(value, by):
        return lax.ppermute(value, "scan", [(i, (i + by) % regions) for i in range(regions)])

    def across(value, flip, by, sections=range(depth)):
        if flip == 0 and by == 0:
            return value
        route = [
            (d * regions + i, (d ^ flip) * regions + (i + by) % regions)
            for d in sections
            for i in range(regions)
        ]
        return lax.ppermute(value, ("depth", "scan"), route)

    smem = pl.BlockSpec(memory_space=pltpu.SMEM)
    vmem = pl.BlockSpec(memory_space=pltpu.VMEM)

    def call(kernel, out_shape, in_specs, flops, name, scratch=()):
        return pl.pallas_call(
            kernel,
            out_shape=out_shape,
            in_specs=in_specs,
            out_specs=jax.tree.map(lambda _: vmem, out_shape),
            scratch_shapes=scratch,
            compiler_params=pltpu.CompilerParams(vmem_limit_bytes=24 * 1024 * 1024),
            cost_estimate=pl.CostEstimate(flops=flops, bytes_accessed=4 << 20, transcendentals=0),
            name=name,
        )

    shape = jax.ShapeDtypeStruct
    piece = shape((count, 2, strip, side), bf16)
    wave = (2, side, side)
    field = (count,) + wave
    left, right = (jnp.asarray(table) for table in tables(side))
    lower = range(depth // 2)

    adjoint = call(
        pick_kernel,
        shape(wave, bf16),
        [pl.BlockSpec(memory_space=pltpu.HBM)],
        1 << 20,
        "pick",
        [pltpu.VMEM(wave, f32), pltpu.SemaphoreType.DMA],
    )(exit_adjoint)
    adjoint, scan_row = lax.optimization_barrier((adjoint, scan_row))
    adjoint = along_scan(adjoint, home)
    packed = scan_row * width + scan_col
    places = [packed] + [along_scan(packed, step) for step in range(1, reach)]

    order = [(flip, step) for flip in range(2) for step in range(reach)]
    far_first = sorted(order, key=lambda key: -abs(key[1] - home))
    pieces = call(
        functools.partial(extract_kernel, reach),
        [piece] * len(order),
        [smem] * reach + [vmem],
        1 << 26,
        "extract",
    )(*places, transmission[0])
    pieces = dict(zip(order, pieces))
    adjoint, pieces[0, home] = lax.optimization_barrier((adjoint, pieces[0, home]))
    adjoints = [adjoint, across(adjoint, 2, 0, lower)]
    for flip, step in far_first:
        pieces[flip, step] = across(pieces[flip, step], flip, home - step)

    start = call(
        functools.partial(start_kernel, home, strip, width),
        shape(field, f32),
        [smem] + [vmem] * (3 + count),
        1 << 30,
        "start",
    )(places[home], probe, *adjoints, left, right)
    chains = []
    for turn in range(count):
        frames, forward, sent = call(
            functools.partial(near_kernel, home, turn, turn == count - 1, width),
            [shape((2,) + wave, bf16), shape(wave, f32), shape(wave, bf16)],
            [smem] + [vmem] * (3 + len(order)),
            1 << 30,
            "near",
        )(places[home], start, left, right, *(pieces[key] for key in order))
        chains.append((frames, forward, across(sent, 2, 0)))
    kept, given, lasts = [], [], []
    for turn, chain in enumerate(chains):
        mine, other, last = call(
            functools.partial(far_kernel, turn, turn == count - 1),
            [shape(wave, bf16)] * 2 + [shape(wave, f32)],
            [vmem] * 6,
            1 << 31,
            "far",
        )(start, left, right, *chain)
        kept.append(mine)
        given.append(across(other, 1, 0))
        lasts.append(last)
    parts = call(
        functools.partial(part_kernel, home, width),
        [shape((2,) + piece.shape, bf16)] * reach,
        [smem] + [vmem] * (2 * count),
        1 << 26,
        "part",
    )(places[home], *kept, *given)
    parts = list(parts)

    height = side // depth
    near, away, probe_sent = call(
        functools.partial(probe_kernel, home, strip, width),
        [shape((2, height, side), f32)] * 2 + [shape((2, 2, height, side), bf16)],
        [smem] + [vmem] * count,
        1 << 26,
        "probe",
        [pltpu.VMEM(wave, f32)],
    )(places[home], *lasts)
    returned = [across(part, 0, step - home) for step, part in enumerate(parts)]

    def scan_round(total, span):
        rounded = total.astype(bf16)
        route = [(i, i ^ span) for i in range(regions)]
        return rounded.astype(f32) + lax.ppermute(rounded, "scan", route).astype(f32)

    def probe_rounds(_, held):
        near, away, given = held
        away = across((away + given[1].astype(f32)).astype(bf16), 2, 0, lower).astype(f32)
        total = jnp.where(half == 0, near + given[0].astype(f32), away)
        for span in spans[:-1]:
            total = scan_round(total, span)
        return total, away, given

    half = lax.axis_index("depth") // (depth // 2)
    once = lax.axis_index("depth") // depth + 1
    assert regions & (regions - 1) == 0
    spans = [1 << level for level in range(regions.bit_length() - 1)]
    near, parts[home] = lax.optimization_barrier((near, parts[home]))
    probe_grad, *_ = lax.fori_loop(
        0, once, probe_rounds, (near, away, across(probe_sent, 1, 0))
    )
    probe_grad, returned = lax.optimization_barrier((probe_grad, returned))
    probe_grad = scan_round(probe_grad, spans[-1])
    object_grad = call(
        functools.partial(deposit_kernel, reach),
        shape(transmission.shape[1:], f32),
        [smem] * reach + [vmem] * reach,
        1 << 26,
        "deposit",
    )(*places, *returned)
    return object_grad[None], probe_grad


def solution(mesh):
    placed = (
        P("depth", None, "scan", None),
        P(),
        P(None, "scan", None, None, None),
        P(None, "scan"),
        P(None, "scan"),
    )
    return jax.shard_map(
        local,
        mesh=mesh,
        in_specs=placed,
        out_specs=(P("depth", None, "scan", None), P(None, "depth", None)),
        check_vma=False,
    )
```

```python
import functools

import jax
import jax.numpy as jnp
import numpy as np
from jax import lax
from jax.experimental import pallas as pl
from jax.experimental.pallas import tpu as pltpu
from jax.sharding import PartitionSpec as P

fresnel = 0.25
LANES = 128
bf16 = jnp.bfloat16
f32 = jnp.float32


def propagator(extent):
    indices = np.arange(extent)
    frequency = np.where(indices < extent // 2, indices, indices - extent).astype(np.float64)
    factor = np.exp(-1j * np.pi * fresnel / extent * frequency * frequency)
    column = np.fft.ifft(factor)
    matrix = column[(indices[:, None] - indices[None, :]) % extent]
    return matrix.real, matrix.imag


def halves(matrix):
    high = matrix.astype(np.float32).astype(bf16)
    low = (matrix - high.astype(np.float64)).astype(np.float32).astype(bf16)
    return high, low


def tables(extent):
    real, imag = propagator(extent)
    left = halves(np.concatenate([real, imag], axis=0))
    right = halves(np.concatenate([real, imag], axis=1))
    left_table = np.concatenate([left[0], left[0], left[1]], axis=1)
    right_table = np.concatenate([right[0], right[0], right[1]], axis=0)
    return left_table, right_table


def split(values):
    high = values.astype(bf16)
    low = (values - high.astype(f32)).astype(bf16)
    return high, low


def propagate(fields, left, right):
    side = fields[0][0].shape[0]

    def parts(values, axis):
        high, low = split(values)
        if left.shape[1] == 3 * side:
            return jnp.concatenate([high, low, high], axis=axis)
        return jnp.concatenate([high, high], axis=axis)

    columns = parts(jnp.concatenate([part for field in fields for part in field], axis=1), 0)
    middle = jnp.dot(left, columns, preferred_element_type=f32)
    rows = []
    for index in range(len(fields)):
        by_real = middle[:side, 2 * index * side : 2 * (index + 1) * side]
        by_imag = middle[side:, 2 * index * side : 2 * (index + 1) * side]
        rows.append(by_real[:, :side] - by_imag[:, side:])
        rows.append(by_real[:, side:] + by_imag[:, :side])
    result = jnp.dot(parts(jnp.concatenate(rows, axis=0), 1), right, preferred_element_type=f32)
    results = []
    for index in range(len(fields)):
        real = result[2 * index * side : (2 * index + 1) * side]
        imag = result[(2 * index + 1) * side : 2 * (index + 1) * side]
        results.append((real[:, :side] - imag[:, side:], real[:, side:] + imag[:, :side]))
    return results


def multiply(first, second):
    return (
        first[0] * second[0] - first[1] * second[1],
        first[0] * second[1] + first[1] * second[0],
    )


def turned(values, down, across):
    return pltpu.roll(pltpu.roll(values, down, 0), across, 1)


def turned_back(values, down, across):
    rows, columns = values.shape
    return turned(values, lax.rem(rows - down, rows), lax.rem(columns - across, columns))


def stretch(column, side, width):
    base = pl.multiple_of(column // LANES * LANES, LANES)
    after = pl.multiple_of(jnp.minimum(base + side, width - LANES), LANES)
    return base, after, column - base


def this_place():
    section = lax.axis_index("depth")
    return section % 2, section // 2


def column_of(places, width, *index):
    return lax.rem(places[index], width)


def window_place(places, home, turn, strip, width, flip=0):
    core, _ = this_place()
    regions = lax.axis_size("scan")
    source = lax.rem(lax.axis_index("scan") - home + regions, regions)
    value = places[core ^ flip, turn]
    return value // width - source * strip, lax.rem(lax.rem(value, width), LANES)


def pick_kernel(waves, out, buffer, arrived):
    core, half = this_place()
    copy = pltpu.make_async_copy(waves.at[core, 1 - half], buffer, arrived)
    copy.start()
    copy.wait()
    out[...] = buffer[...].astype(bf16)


def extract_kernel(reach, *refs):
    places, (strip, *outs) = refs[:reach], refs[reach:]
    count, _, rows, side = outs[0].shape
    width = strip.shape[2]
    core, _ = this_place()
    lane = lax.broadcasted_iota(jnp.int32, (rows, LANES), 1)
    for flip in range(2):
        for step in range(reach):
            out = outs[flip * reach + step]
            for turn in range(count):
                column = column_of(places[step], width, core ^ flip, turn)
                base, after, begin = stretch(column, side, width)
                rest = pl.multiple_of(base + LANES, LANES)
                for plane in range(2):
                    first = strip[plane, :, pl.ds(base, LANES)]
                    again = strip[plane, :, pl.ds(after, LANES)]
                    out[turn, plane, :, :LANES] = jnp.where(lane < begin, again, first).astype(bf16)
                    out[turn, plane, :, LANES:] = strip[plane, :, pl.ds(rest, side - LANES)].astype(
                        bf16
                    )


def start_kernel(home, strip, width, places, probe, *refs):
    adjoints, (left, right, out) = refs[:-3], refs[-3:]
    _, half = this_place()

    @pl.when(half == 0)
    def _():
        for turn in range(len(adjoints)):
            down, across = window_place(places, home, turn, strip, width)
            for plane in range(2):
                out[turn, plane] = turned(probe[plane], down, across)

    @pl.when(half != 0)
    def _():
        fields = []
        for turn, adjoint in enumerate(adjoints):
            down, across = window_place(places, home, turn, strip, width)
            real, imag = (turned(adjoint[plane].astype(f32), down, across) for plane in range(2))
            fields.append((real, -imag))
        for turn, field in enumerate(propagate(fields, left[...], right[...])):
            out[turn, 0], out[turn, 1] = field


def pair(ref, *index):
    return ref[(*index, 0)].astype(f32), ref[(*index, 1)].astype(f32)


def own_first():
    core, half = this_place()
    return jnp.where(core == half, 0, 1)


def near_kernel(home, turn, early, width, places, start, left, right, *refs):
    pieces, (frames, wave, sent) = refs[:-3], refs[-3:]
    reach = len(pieces) // 2
    _, _, strip, side = pieces[0].shape
    own = own_first()
    row = lax.broadcasted_iota(jnp.int32, (strip, side), 0)
    down, _ = window_place(places, home, turn, strip, width)
    for flip in range(2):
        parts = pieces[flip * reach : (flip + 1) * reach]
        for plane in range(2):
            first = parts[0][turn, plane].astype(f32)
            again = parts[-1][turn, plane].astype(f32)
            frames[own ^ flip, plane, :strip] = jnp.where(row < down, again, first).astype(bf16)
            for step in range(1, reach - 1):
                frames[own ^ flip, plane, step * strip : (step + 1) * strip] = parts[step][
                    turn, plane
                ]
    field = multiply(pair(frames, 0), pair(start, turn))
    if early:
        (field,) = propagate([field], left[:, side:], right[side:])
        wave[0], wave[1] = field
        real, imag = multiply(pair(frames, 1), field)
    else:
        (field,) = propagate([field], left[...], right[...])
        wave[0], wave[1] = field
        ((real, imag),) = propagate([multiply(pair(frames, 1), field)], left[...], right[...])
    sent[0] = real.astype(bf16)
    sent[1] = imag.astype(bf16)


def far_kernel(turn, early, start, left, right, frames, wave, arrived, kept, given, last):
    own = own_first()
    side = start.shape[2]
    field = pair(arrived)
    if early:
        (field,) = propagate([field], left[...], right[...])
        outer = multiply(pair(wave), field)
        (field,) = propagate([multiply(pair(frames, 1), field)], left[...], right[...])
    else:
        outer = multiply(pair(wave), field)
        (field,) = propagate([multiply(pair(frames, 1), field)], left[:, side:], right[side:])
    first = multiply(pair(start, turn), field)
    for plane, sign in ((0, 1.0), (1, -1.0)):
        kept[plane] = (jnp.where(own == 0, first[plane], outer[plane]) * sign).astype(bf16)
        given[plane] = (jnp.where(own == 0, outer[plane], first[plane]) * sign).astype(bf16)
    last[0], last[1] = multiply(pair(frames, 0), field)


def part_kernel(home, width, places, *refs):
    count = places.shape[1]
    windows, outs = refs[: 2 * count], refs[2 * count :]
    _, _, _, strip, side = outs[0].shape
    row = lax.broadcasted_iota(jnp.int32, (strip, side), 0)
    for flip in range(2):
        for turn in range(count):
            window = windows[flip * count + turn]
            down, _ = window_place(places, home, turn, strip, width, flip)
            for plane in range(2):
                ends = window[plane, :strip].astype(f32)
                outs[0][flip, turn, plane] = jnp.where(row < down, 0.0, ends).astype(bf16)
                outs[-1][flip, turn, plane] = jnp.where(row < down, ends, 0.0).astype(bf16)
                for step in range(1, len(outs) - 1):
                    outs[step][flip, turn, plane] = window[
                        plane, step * strip : (step + 1) * strip
                    ]


def probe_kernel(home, strip, width, places, *refs):
    waves, (near, away, sent, total) = refs[:-4], refs[-4:]
    core, half = this_place()
    weight = jnp.where(half == 0, 1.0, 0.0)
    for plane, sign in ((0, weight), (1, -weight)):
        parts = []
        for turn, wave in enumerate(waves):
            down, across = window_place(places, home, turn, strip, width)
            parts.append(turned_back(wave[plane], down, across))
        total[plane] = sum(parts) * sign
    height = near.shape[1]
    for index, out in enumerate((near, away)):
        for plane in range(2):
            mine = pl.multiple_of((2 * index + core) * height, height)
            other = pl.multiple_of((2 * index + (core ^ 1)) * height, height)
            out[plane] = total[plane, pl.ds(mine, height)]
            sent[index, plane] = total[plane, pl.ds(other, height)].astype(bf16)


def deposit_kernel(reach, *refs):
    places, pieces, out = refs[:reach], refs[reach:-1], refs[-1]
    _, count, _, strip, side = pieces[0].shape
    width = out.shape[2]
    core, _ = this_place()
    lane = lax.broadcasted_iota(jnp.int32, (strip, LANES), 1)
    out[...] = jnp.zeros(out.shape, f32)
    for step, piece in enumerate(pieces):
        for flip in range(2):
            for turn in range(count):
                column = column_of(places[step], width, core ^ flip, turn)
                base, after, begin = stretch(column, side, width)
                rest = pl.multiple_of(base + LANES, LANES)
                for plane in range(2):
                    ends = piece[flip, turn, plane, :, :LANES].astype(f32)
                    out[plane, :, pl.ds(base, LANES)] += jnp.where(lane < begin, 0.0, ends)
                    out[plane, :, pl.ds(rest, side - LANES)] += piece[
                        flip, turn, plane, :, LANES:
                    ].astype(f32)
                    out[plane, :, pl.ds(after, LANES)] += jnp.where(lane < begin, ends, 0.0)


def local(transmission, probe, exit_adjoint, scan_row, scan_col):
    depth = lax.axis_size("depth")
    regions = lax.axis_size("scan")
    strip, width = transmission.shape[2:]
    side = probe.shape[1]
    reach = side // strip + 1
    home = reach // 2
    count = scan_row.shape[1]
    assert transmission.shape[0] == 1 and depth == 4 and scan_row.shape[0] == 2
    assert side == 2 * LANES and count == 2

    def along_scan(value, by):
        return lax.ppermute(value, "scan", [(i, (i + by) % regions) for i in range(regions)])

    def across(value, flip, by, sections=range(depth)):
        if flip == 0 and by == 0:
            return value
        route = [
            (d * regions + i, (d ^ flip) * regions + (i + by) % regions)
            for d in sections
            for i in range(regions)
        ]
        return lax.ppermute(value, ("depth", "scan"), route)

    smem = pl.BlockSpec(memory_space=pltpu.SMEM)
    vmem = pl.BlockSpec(memory_space=pltpu.VMEM)

    def call(kernel, out_shape, in_specs, flops, name, scratch=()):
        return pl.pallas_call(
            kernel,
            out_shape=out_shape,
            in_specs=in_specs,
            out_specs=jax.tree.map(lambda _: vmem, out_shape),
            scratch_shapes=scratch,
            compiler_params=pltpu.CompilerParams(vmem_limit_bytes=24 * 1024 * 1024),
            cost_estimate=pl.CostEstimate(flops=flops, bytes_accessed=4 << 20, transcendentals=0),
            name=name,
        )

    shape = jax.ShapeDtypeStruct
    piece = shape((count, 2, strip, side), bf16)
    wave = (2, side, side)
    field = (count,) + wave
    left, right = (jnp.asarray(table) for table in tables(side))
    lower = range(depth // 2)

    adjoint = call(
        pick_kernel,
        shape(wave, bf16),
        [pl.BlockSpec(memory_space=pltpu.HBM)],
        1 << 20,
        "pick",
        [pltpu.VMEM(wave, f32), pltpu.SemaphoreType.DMA],
    )(exit_adjoint)
    adjoint, scan_row = lax.optimization_barrier((adjoint, scan_row))
    adjoint = along_scan(adjoint, home)
    packed = scan_row * width + scan_col
    places = [packed] + [along_scan(packed, step) for step in range(1, reach)]

    order = [(flip, step) for flip in range(2) for step in range(reach)]
    far_first = sorted(order, key=lambda key: -abs(key[1] - home))
    pieces = call(
        functools.partial(extract_kernel, reach),
        [piece] * len(order),
        [smem] * reach + [vmem],
        1 << 26,
        "extract",
    )(*places, transmission[0])
    pieces = dict(zip(order, pieces))
    adjoint, pieces[0, home] = lax.optimization_barrier((adjoint, pieces[0, home]))
    adjoints = [adjoint, across(adjoint, 2, 0, lower)]
    for flip, step in far_first:
        if (flip, step) == (1, home):
            pieces[1, home], pieces[0, 0] = lax.optimization_barrier((pieces[1, home], pieces[0, 0]))
        pieces[flip, step] = across(pieces[flip, step], flip, home - step)

    start = call(
        functools.partial(start_kernel, home, strip, width),
        shape(field, f32),
        [smem] + [vmem] * (3 + count),
        1 << 30,
        "start",
    )(places[home], probe, *adjoints, left, right)
    chains = []
    for turn in range(count):
        frames, forward, sent = call(
            functools.partial(near_kernel, home, turn, turn == count - 1, width),
            [shape((2,) + wave, bf16), shape(wave, f32), shape(wave, bf16)],
            [smem] + [vmem] * (3 + len(order)),
            1 << 30,
            "near",
        )(places[home], start, left, right, *(pieces[key] for key in order))
        chains.append((frames, forward, across(sent, 2, 0)))
    kept, given, lasts = [], [], []
    for turn, chain in enumerate(chains):
        mine, other, last = call(
            functools.partial(far_kernel, turn, turn == count - 1),
            [shape(wave, bf16)] * 2 + [shape(wave, f32)],
            [vmem] * 6,
            1 << 31,
            "far",
        )(start, left, right, *chain)
        kept.append(mine)
        given.append(across(other, 1, 0))
        lasts.append(last)
    parts = call(
        functools.partial(part_kernel, home, width),
        [shape((2,) + piece.shape, bf16)] * reach,
        [smem] + [vmem] * (2 * count),
        1 << 26,
        "part",
    )(places[home], *kept, *given)
    parts = list(parts)

    height = side // depth
    near, away, probe_sent = call(
        functools.partial(probe_kernel, home, strip, width),
        [shape((2, height, side), f32)] * 2 + [shape((2, 2, height, side), bf16)],
        [smem] + [vmem] * count,
        1 << 26,
        "probe",
        [pltpu.VMEM(wave, f32)],
    )(places[home], *lasts)
    returned = [across(part, 0, step - home) for step, part in enumerate(parts)]

    def scan_round(total, span):
        rounded = total.astype(bf16)
        route = [(i, i ^ span) for i in range(regions)]
        return rounded.astype(f32) + lax.ppermute(rounded, "scan", route).astype(f32)

    half = lax.axis_index("depth") // (depth // 2)
    once = lax.axis_index("depth") // depth + 1
    assert regions & (regions - 1) == 0
    spans = [1 << level for level in range(regions.bit_length() - 1)]
    given = across(probe_sent, 1, 0)
    away = (away + given[1].astype(f32)).astype(bf16)
    away, parts[home] = lax.optimization_barrier((away, parts[home]))

    def probe_rounds(_, held):
        near, given, away = held
        total = jnp.where(half == 0, near + given[0].astype(f32), away.astype(f32))
        for span in spans[:-1]:
            total = scan_round(total, span)
        return total, given, away

    probe_grad, *_ = lax.fori_loop(
        0, once, probe_rounds, (near, given, across(away, 2, 0, lower))
    )
    probe_grad, returned = lax.optimization_barrier((probe_grad, returned))
    probe_grad = scan_round(probe_grad, spans[-1])
    object_grad = call(
        functools.partial(deposit_kernel, reach),
        shape(transmission.shape[1:], f32),
        [smem] * reach + [vmem] * reach,
        1 << 26,
        "deposit",
    )(*places, *returned)
    return object_grad[None], probe_grad


def solution(mesh):
    placed = (
        P("depth", None, "scan", None),
        P(),
        P(None, "scan", None, None, None),
        P(None, "scan"),
        P(None, "scan"),
    )
    return jax.shard_map(
        local,
        mesh=mesh,
        in_specs=placed,
        out_specs=(P("depth", None, "scan", None), P(None, "depth", None)),
        check_vma=False,
    )
```

```python
import functools

import jax
import jax.numpy as jnp
import numpy as np
from jax import lax
from jax.experimental import pallas as pl
from jax.experimental.pallas import tpu as pltpu
from jax.sharding import PartitionSpec as P

fresnel = 0.25
LANES = 128
bf16 = jnp.bfloat16
f32 = jnp.float32


def propagator(extent):
    indices = np.arange(extent)
    frequency = np.where(indices < extent // 2, indices, indices - extent).astype(np.float64)
    factor = np.exp(-1j * np.pi * fresnel / extent * frequency * frequency)
    column = np.fft.ifft(factor)
    matrix = column[(indices[:, None] - indices[None, :]) % extent]
    return matrix.real, matrix.imag


def halves(matrix):
    high = matrix.astype(np.float32).astype(bf16)
    low = (matrix - high.astype(np.float64)).astype(np.float32).astype(bf16)
    return high, low


def tables(extent):
    real, imag = propagator(extent)
    left = halves(np.concatenate([real, imag], axis=0))
    right = halves(np.concatenate([real, imag], axis=1))
    left_table = np.concatenate([left[0], left[0], left[1]], axis=1)
    right_table = np.concatenate([right[0], right[0], right[1]], axis=0)
    return left_table, right_table


def split(values):
    high = values.astype(bf16)
    low = (values - high.astype(f32)).astype(bf16)
    return high, low


def propagate(fields, left, right):
    side = fields[0][0].shape[0]

    def parts(values, axis):
        high, low = split(values)
        if left.shape[1] == 3 * side:
            return jnp.concatenate([high, low, high], axis=axis)
        return jnp.concatenate([high, high], axis=axis)

    columns = parts(jnp.concatenate([part for field in fields for part in field], axis=1), 0)
    middle = jnp.dot(left, columns, preferred_element_type=f32)
    rows = []
    for index in range(len(fields)):
        by_real = middle[:side, 2 * index * side : 2 * (index + 1) * side]
        by_imag = middle[side:, 2 * index * side : 2 * (index + 1) * side]
        rows.append(by_real[:, :side] - by_imag[:, side:])
        rows.append(by_real[:, side:] + by_imag[:, :side])
    result = jnp.dot(parts(jnp.concatenate(rows, axis=0), 1), right, preferred_element_type=f32)
    results = []
    for index in range(len(fields)):
        real = result[2 * index * side : (2 * index + 1) * side]
        imag = result[(2 * index + 1) * side : 2 * (index + 1) * side]
        results.append((real[:, :side] - imag[:, side:], real[:, side:] + imag[:, :side]))
    return results


def multiply(first, second):
    return (
        first[0] * second[0] - first[1] * second[1],
        first[0] * second[1] + first[1] * second[0],
    )


def turned(values, down, across):
    return pltpu.roll(pltpu.roll(values, down, 0), across, 1)


def turned_back(values, down, across):
    rows, columns = values.shape
    return turned(values, lax.rem(rows - down, rows), lax.rem(columns - across, columns))


def stretch(column, side, width):
    base = pl.multiple_of(column // LANES * LANES, LANES)
    after = pl.multiple_of(jnp.minimum(base + side, width - LANES), LANES)
    return base, after, column - base


def this_place():
    section = lax.axis_index("depth")
    return section % 2, section // 2


def column_of(places, width, *index):
    return lax.rem(places[index], width)


def window_place(places, home, turn, strip, width, flip=0):
    core, _ = this_place()
    regions = lax.axis_size("scan")
    source = lax.rem(lax.axis_index("scan") - home + regions, regions)
    value = places[core ^ flip, turn]
    return value // width - source * strip, lax.rem(lax.rem(value, width), LANES)


def pick_kernel(waves, out, buffer, arrived):
    core, half = this_place()
    copy = pltpu.make_async_copy(waves.at[core, 1 - half], buffer, arrived)
    copy.start()
    copy.wait()
    out[...] = buffer[...].astype(bf16)


def extract_kernel(reach, *refs):
    places, (strip, *outs) = refs[:reach], refs[reach:]
    count, _, rows, side = outs[0].shape
    width = strip.shape[2]
    core, _ = this_place()
    lane = lax.broadcasted_iota(jnp.int32, (rows, LANES), 1)
    for flip in range(2):
        for step in range(reach):
            out = outs[flip * reach + step]
            for turn in range(count):
                column = column_of(places[step], width, core ^ flip, turn)
                base, after, begin = stretch(column, side, width)
                rest = pl.multiple_of(base + LANES, LANES)
                for plane in range(2):
                    first = strip[plane, :, pl.ds(base, LANES)]
                    again = strip[plane, :, pl.ds(after, LANES)]
                    out[turn, plane, :, :LANES] = jnp.where(lane < begin, again, first).astype(bf16)
                    out[turn, plane, :, LANES:] = strip[plane, :, pl.ds(rest, side - LANES)].astype(
                        bf16
                    )


def start_kernel(home, strip, width, places, probe, *refs):
    adjoints, (left, right, out) = refs[:-3], refs[-3:]
    _, half = this_place()

    @pl.when(half == 0)
    def _():
        for turn in range(len(adjoints)):
            down, across = window_place(places, home, turn, strip, width)
            for plane in range(2):
                out[turn, plane] = turned(probe[plane], down, across)

    @pl.when(half != 0)
    def _():
        fields = []
        for turn, adjoint in enumerate(adjoints):
            down, across = window_place(places, home, turn, strip, width)
            real, imag = (turned(adjoint[plane].astype(f32), down, across) for plane in range(2))
            fields.append((real, -imag))
        for turn, field in enumerate(propagate(fields, left[...], right[...])):
            out[turn, 0], out[turn, 1] = field


def pair(ref, *index):
    return ref[(*index, 0)].astype(f32), ref[(*index, 1)].astype(f32)


def own_first():
    core, half = this_place()
    return jnp.where(core == half, 0, 1)


def near_kernel(home, turn, early, width, places, start, left, right, *refs):
    pieces, (frames, wave, sent) = refs[:-3], refs[-3:]
    reach = len(pieces) // 2
    _, _, strip, side = pieces[0].shape
    own = own_first()
    row = lax.broadcasted_iota(jnp.int32, (strip, side), 0)
    down, _ = window_place(places, home, turn, strip, width)
    for flip in range(2):
        parts = pieces[flip * reach : (flip + 1) * reach]
        for plane in range(2):
            first = parts[0][turn, plane].astype(f32)
            again = parts[-1][turn, plane].astype(f32)
            frames[own ^ flip, plane, :strip] = jnp.where(row < down, again, first).astype(bf16)
            for step in range(1, reach - 1):
                frames[own ^ flip, plane, step * strip : (step + 1) * strip] = parts[step][
                    turn, plane
                ]
    field = multiply(pair(frames, 0), pair(start, turn))
    if early:
        (field,) = propagate([field], left[:, side:], right[side:])
        wave[0], wave[1] = field
        real, imag = multiply(pair(frames, 1), field)
    else:
        (field,) = propagate([field], left[...], right[...])
        wave[0], wave[1] = field
        ((real, imag),) = propagate([multiply(pair(frames, 1), field)], left[...], right[...])
    sent[0] = real.astype(bf16)
    sent[1] = imag.astype(bf16)


def far_kernel(turn, early, start, left, right, frames, wave, arrived, kept, given, last):
    own = own_first()
    side = start.shape[2]
    field = pair(arrived)
    if early:
        (field,) = propagate([field], left[...], right[...])
        outer = multiply(pair(wave), field)
        (field,) = propagate([multiply(pair(frames, 1), field)], left[...], right[...])
    else:
        outer = multiply(pair(wave), field)
        (field,) = propagate([multiply(pair(frames, 1), field)], left[:, side:], right[side:])
    first = multiply(pair(start, turn), field)
    for plane, sign in ((0, 1.0), (1, -1.0)):
        kept[plane] = (jnp.where(own == 0, first[plane], outer[plane]) * sign).astype(bf16)
        given[plane] = (jnp.where(own == 0, outer[plane], first[plane]) * sign).astype(bf16)
    last[0], last[1] = multiply(pair(frames, 0), field)


def part_kernel(home, width, places, *refs):
    count = places.shape[1]
    windows, outs = refs[: 2 * count], refs[2 * count :]
    _, _, _, strip, side = outs[0].shape
    row = lax.broadcasted_iota(jnp.int32, (strip, side), 0)
    for flip in range(2):
        for turn in range(count):
            window = windows[flip * count + turn]
            down, _ = window_place(places, home, turn, strip, width, flip)
            for plane in range(2):
                ends = window[plane, :strip].astype(f32)
                outs[0][flip, turn, plane] = jnp.where(row < down, 0.0, ends).astype(bf16)
                outs[-1][flip, turn, plane] = jnp.where(row < down, ends, 0.0).astype(bf16)
                for step in range(1, len(outs) - 1):
                    outs[step][flip, turn, plane] = window[
                        plane, step * strip : (step + 1) * strip
                    ]


def probe_kernel(home, strip, width, places, *refs):
    waves, (near, away, sent, total) = refs[:-4], refs[-4:]
    core, half = this_place()
    weight = jnp.where(half == 0, 1.0, 0.0)
    for plane, sign in ((0, weight), (1, -weight)):
        parts = []
        for turn, wave in enumerate(waves):
            down, across = window_place(places, home, turn, strip, width)
            parts.append(turned_back(wave[plane], down, across))
        total[plane] = sum(parts) * sign
    height = near.shape[1]
    for index, out in enumerate((near, away)):
        for plane in range(2):
            mine = pl.multiple_of((2 * index + core) * height, height)
            other = pl.multiple_of((2 * index + (core ^ 1)) * height, height)
            out[plane] = total[plane, pl.ds(mine, height)]
            sent[index, plane] = total[plane, pl.ds(other, height)].astype(bf16)


def deposit_kernel(reach, *refs):
    places, pieces, out = refs[:reach], refs[reach:-1], refs[-1]
    _, count, _, strip, side = pieces[0].shape
    width = out.shape[2]
    core, _ = this_place()
    lane = lax.broadcasted_iota(jnp.int32, (strip, LANES), 1)
    out[...] = jnp.zeros(out.shape, f32)
    for step, piece in enumerate(pieces):
        for flip in range(2):
            for turn in range(count):
                column = column_of(places[step], width, core ^ flip, turn)
                base, after, begin = stretch(column, side, width)
                rest = pl.multiple_of(base + LANES, LANES)
                for plane in range(2):
                    ends = piece[flip, turn, plane, :, :LANES].astype(f32)
                    out[plane, :, pl.ds(base, LANES)] += jnp.where(lane < begin, 0.0, ends)
                    out[plane, :, pl.ds(rest, side - LANES)] += piece[
                        flip, turn, plane, :, LANES:
                    ].astype(f32)
                    out[plane, :, pl.ds(after, LANES)] += jnp.where(lane < begin, ends, 0.0)


def local(transmission, probe, exit_adjoint, scan_row, scan_col):
    depth = lax.axis_size("depth")
    regions = lax.axis_size("scan")
    strip, width = transmission.shape[2:]
    side = probe.shape[1]
    reach = side // strip + 1
    home = reach // 2
    count = scan_row.shape[1]
    assert transmission.shape[0] == 1 and depth == 4 and scan_row.shape[0] == 2
    assert side == 2 * LANES and count == 2

    def along_scan(value, by):
        return lax.ppermute(value, "scan", [(i, (i + by) % regions) for i in range(regions)])

    def across(value, flip, by, sections=range(depth)):
        if flip == 0 and by == 0:
            return value
        route = [
            (d * regions + i, (d ^ flip) * regions + (i + by) % regions)
            for d in sections
            for i in range(regions)
        ]
        return lax.ppermute(value, ("depth", "scan"), route)

    smem = pl.BlockSpec(memory_space=pltpu.SMEM)
    vmem = pl.BlockSpec(memory_space=pltpu.VMEM)

    def call(kernel, out_shape, in_specs, flops, name, scratch=(), limit=24):
        return pl.pallas_call(
            kernel,
            out_shape=out_shape,
            in_specs=in_specs,
            out_specs=jax.tree.map(lambda _: vmem, out_shape),
            scratch_shapes=scratch,
            compiler_params=pltpu.CompilerParams(vmem_limit_bytes=limit << 20),
            cost_estimate=pl.CostEstimate(flops=flops, bytes_accessed=4 << 20, transcendentals=0),
            name=name,
        )

    shape = jax.ShapeDtypeStruct
    piece = shape((count, 2, strip, side), bf16)
    wave = (2, side, side)
    field = (count,) + wave
    left, right = (jnp.asarray(table) for table in tables(side))
    lower = range(depth // 2)

    adjoint = call(
        pick_kernel,
        shape(wave, bf16),
        [pl.BlockSpec(memory_space=pltpu.HBM)],
        1 << 20,
        "pick",
        [pltpu.VMEM(wave, f32), pltpu.SemaphoreType.DMA],
        62,
    )(exit_adjoint)
    adjoint, scan_row = lax.optimization_barrier((adjoint, scan_row))
    adjoint = along_scan(adjoint, home)
    packed = scan_row * width + scan_col
    places = [packed] + [along_scan(packed, step) for step in range(1, reach)]

    order = [(flip, step) for flip in range(2) for step in range(reach)]
    far_first = sorted(order, key=lambda key: -abs(key[1] - home))
    pieces = call(
        functools.partial(extract_kernel, reach),
        [piece] * len(order),
        [smem] * reach + [vmem],
        1 << 26,
        "extract",
    )(*places, transmission[0])
    pieces = dict(zip(order, pieces))
    adjoint, pieces[0, home] = lax.optimization_barrier((adjoint, pieces[0, home]))
    adjoints = [adjoint, across(adjoint, 2, 0, lower)]
    for flip, step in far_first:
        if (flip, step) == (1, home):
            pieces[1, home], pieces[0, 0] = lax.optimization_barrier((pieces[1, home], pieces[0, 0]))
        pieces[flip, step] = across(pieces[flip, step], flip, home - step)

    start = call(
        functools.partial(start_kernel, home, strip, width),
        shape(field, f32),
        [smem] + [vmem] * (3 + count),
        1 << 30,
        "start",
    )(places[home], probe, *adjoints, left, right)
    chains = []
    for turn in range(count):
        frames, forward, sent = call(
            functools.partial(near_kernel, home, turn, turn == count - 1, width),
            [shape((2,) + wave, bf16), shape(wave, f32), shape(wave, bf16)],
            [smem] + [vmem] * (3 + len(order)),
            1 << 30,
            "near",
        )(places[home], start, left, right, *(pieces[key] for key in order))
        chains.append((frames, forward, across(sent, 2, 0)))
    kept, given, lasts = [], [], []
    for turn, chain in enumerate(chains):
        mine, other, last = call(
            functools.partial(far_kernel, turn, turn == count - 1),
            [shape(wave, bf16)] * 2 + [shape(wave, f32)],
            [vmem] * 6,
            1 << 31,
            "far",
        )(start, left, right, *chain)
        kept.append(mine)
        given.append(across(other, 1, 0))
        lasts.append(last)
    parts = call(
        functools.partial(part_kernel, home, width),
        [shape((2,) + piece.shape, bf16)] * reach,
        [smem] + [vmem] * (2 * count),
        1 << 26,
        "part",
    )(places[home], *kept, *given)
    parts = list(parts)

    height = side // depth
    near, away, probe_sent = call(
        functools.partial(probe_kernel, home, strip, width),
        [shape((2, height, side), f32)] * 2 + [shape((2, 2, height, side), bf16)],
        [smem] + [vmem] * count,
        1 << 26,
        "probe",
        [pltpu.VMEM(wave, f32)],
    )(places[home], *lasts)
    returned = [across(part, 0, step - home) for step, part in enumerate(parts)]

    def scan_round(total, span):
        rounded = total.astype(bf16)
        route = [(i, i ^ span) for i in range(regions)]
        return rounded.astype(f32) + lax.ppermute(rounded, "scan", route).astype(f32)

    def probe_rounds(_, held):
        near, away, given = held
        away = across((away + given[1].astype(f32)).astype(bf16), 2, 0, lower).astype(f32)
        total = jnp.where(half == 0, near + given[0].astype(f32), away)
        for span in spans[:-1]:
            total = scan_round(total, span)
        return total, away, given

    half = lax.axis_index("depth") // (depth // 2)
    once = lax.axis_index("depth") // depth + 1
    assert regions & (regions - 1) == 0
    spans = [1 << level for level in range(regions.bit_length() - 1)]
    near, parts[home] = lax.optimization_barrier((near, parts[home]))
    probe_grad, *_ = lax.fori_loop(
        0, once, probe_rounds, (near, away, across(probe_sent, 1, 0))
    )
    probe_grad, returned = lax.optimization_barrier((probe_grad, returned))
    probe_grad = scan_round(probe_grad, spans[-1])
    object_grad = call(
        functools.partial(deposit_kernel, reach),
        shape(transmission.shape[1:], f32),
        [smem] * reach + [vmem] * reach,
        1 << 26,
        "deposit",
    )(*places, *returned)
    return object_grad[None], probe_grad


def solution(mesh):
    placed = (
        P("depth", None, "scan", None),
        P(),
        P(None, "scan", None, None, None),
        P(None, "scan"),
        P(None, "scan"),
    )
    return jax.shard_map(
        local,
        mesh=mesh,
        in_specs=placed,
        out_specs=(P("depth", None, "scan", None), P(None, "depth", None)),
        check_vma=False,
    )
```

```python
import functools

import jax
import jax.numpy as jnp
import numpy as np
from jax import lax
from jax.experimental import pallas as pl
from jax.experimental.pallas import tpu as pltpu
from jax.sharding import PartitionSpec as P

fresnel = 0.25
LANES = 128
bf16 = jnp.bfloat16
f32 = jnp.float32


def propagator(extent):
    indices = np.arange(extent)
    frequency = np.where(indices < extent // 2, indices, indices - extent).astype(np.float64)
    factor = np.exp(-1j * np.pi * fresnel / extent * frequency * frequency)
    column = np.fft.ifft(factor)
    matrix = column[(indices[:, None] - indices[None, :]) % extent]
    return matrix.real, matrix.imag


def halves(matrix):
    high = matrix.astype(np.float32).astype(bf16)
    low = (matrix - high.astype(np.float64)).astype(np.float32).astype(bf16)
    return high, low


def tables(extent):
    real, imag = propagator(extent)
    left = halves(np.concatenate([real, imag], axis=0))
    right = halves(np.concatenate([real, imag], axis=1))
    left_table = np.concatenate([left[0], left[0], left[1]], axis=1)
    right_table = np.concatenate([right[0], right[0], right[1]], axis=0)
    return left_table, right_table


def split(values):
    high = values.astype(bf16)
    low = (values - high.astype(f32)).astype(bf16)
    return high, low


def propagate(fields, left, right):
    side = fields[0][0].shape[0]

    def parts(values, axis):
        high, low = split(values)
        if left.shape[1] == 3 * side:
            return jnp.concatenate([high, low, high], axis=axis)
        return jnp.concatenate([high, high], axis=axis)

    columns = parts(jnp.concatenate([part for field in fields for part in field], axis=1), 0)
    middle = jnp.dot(left, columns, preferred_element_type=f32)
    rows = []
    for index in range(len(fields)):
        by_real = middle[:side, 2 * index * side : 2 * (index + 1) * side]
        by_imag = middle[side:, 2 * index * side : 2 * (index + 1) * side]
        rows.append(by_real[:, :side] - by_imag[:, side:])
        rows.append(by_real[:, side:] + by_imag[:, :side])
    result = jnp.dot(parts(jnp.concatenate(rows, axis=0), 1), right, preferred_element_type=f32)
    results = []
    for index in range(len(fields)):
        real = result[2 * index * side : (2 * index + 1) * side]
        imag = result[(2 * index + 1) * side : 2 * (index + 1) * side]
        results.append((real[:, :side] - imag[:, side:], real[:, side:] + imag[:, :side]))
    return results


def multiply(first, second):
    return (
        first[0] * second[0] - first[1] * second[1],
        first[0] * second[1] + first[1] * second[0],
    )


def turned(values, down, across):
    return pltpu.roll(pltpu.roll(values, down, 0), across, 1)


def turned_back(values, down, across):
    rows, columns = values.shape
    return turned(values, lax.rem(rows - down, rows), lax.rem(columns - across, columns))


def stretch(column, side, width):
    base = pl.multiple_of(column // LANES * LANES, LANES)
    after = pl.multiple_of(jnp.minimum(base + side, width - LANES), LANES)
    return base, after, column - base


def this_place():
    section = lax.axis_index("depth")
    return section % 2, section // 2


def column_of(places, width, *index):
    return lax.rem(places[index], width)


def window_place(places, home, turn, strip, width, flip=0):
    core, _ = this_place()
    regions = lax.axis_size("scan")
    source = lax.rem(lax.axis_index("scan") - home + regions, regions)
    value = places[core ^ flip, turn]
    return value // width - source * strip, lax.rem(lax.rem(value, width), LANES)


def pick_kernel(waves, out, buffer, arrived):
    core, half = this_place()
    planes, rows, _ = out.shape
    height = rows // 2
    copies = []
    for plane in range(planes):
        for start in range(0, rows, height):
            part = (plane, pl.ds(start, height))
            copy = pltpu.make_async_copy(
                waves.at[(core, 1 - half, *part)], buffer.at[part], arrived.at[len(copies)]
            )
            copy.start()
            copies.append((part, copy))
    for part, copy in copies:
        copy.wait()
        out[part] = buffer[part].astype(bf16)


def extract_kernel(reach, *refs):
    places, (strip, *outs) = refs[:reach], refs[reach:]
    count, _, rows, side = outs[0].shape
    width = strip.shape[2]
    core, _ = this_place()
    lane = lax.broadcasted_iota(jnp.int32, (rows, LANES), 1)
    for flip in range(2):
        for step in range(reach):
            out = outs[flip * reach + step]
            for turn in range(count):
                column = column_of(places[step], width, core ^ flip, turn)
                base, after, begin = stretch(column, side, width)
                rest = pl.multiple_of(base + LANES, LANES)
                for plane in range(2):
                    first = strip[plane, :, pl.ds(base, LANES)]
                    again = strip[plane, :, pl.ds(after, LANES)]
                    out[turn, plane, :, :LANES] = jnp.where(lane < begin, again, first).astype(bf16)
                    out[turn, plane, :, LANES:] = strip[plane, :, pl.ds(rest, side - LANES)].astype(
                        bf16
                    )


def start_kernel(home, strip, width, places, probe, *refs):
    adjoints, (left, right, out) = refs[:-3], refs[-3:]
    _, half = this_place()

    @pl.when(half == 0)
    def _():
        for turn in range(len(adjoints)):
            down, across = window_place(places, home, turn, strip, width)
            for plane in range(2):
                out[turn, plane] = turned(probe[plane], down, across)

    @pl.when(half != 0)
    def _():
        fields = []
        for turn, adjoint in enumerate(adjoints):
            down, across = window_place(places, home, turn, strip, width)
            real, imag = (turned(adjoint[plane].astype(f32), down, across) for plane in range(2))
            fields.append((real, -imag))
        for turn, field in enumerate(propagate(fields, left[...], right[...])):
            out[turn, 0], out[turn, 1] = field


def pair(ref, *index):
    return ref[(*index, 0)].astype(f32), ref[(*index, 1)].astype(f32)


def own_first():
    core, half = this_place()
    return jnp.where(core == half, 0, 1)


def near_kernel(home, turn, early, width, places, start, left, right, *refs):
    pieces, (frames, wave, sent) = refs[:-3], refs[-3:]
    reach = len(pieces) // 2
    _, _, strip, side = pieces[0].shape
    own = own_first()
    row = lax.broadcasted_iota(jnp.int32, (strip, side), 0)
    down, _ = window_place(places, home, turn, strip, width)
    for flip in range(2):
        parts = pieces[flip * reach : (flip + 1) * reach]
        for plane in range(2):
            first = parts[0][turn, plane].astype(f32)
            again = parts[-1][turn, plane].astype(f32)
            frames[own ^ flip, plane, :strip] = jnp.where(row < down, again, first).astype(bf16)
            for step in range(1, reach - 1):
                frames[own ^ flip, plane, step * strip : (step + 1) * strip] = parts[step][
                    turn, plane
                ]
    field = multiply(pair(frames, 0), pair(start, turn))
    if early:
        (field,) = propagate([field], left[:, side:], right[side:])
        wave[0], wave[1] = field
        real, imag = multiply(pair(frames, 1), field)
    else:
        (field,) = propagate([field], left[...], right[...])
        wave[0], wave[1] = field
        ((real, imag),) = propagate([multiply(pair(frames, 1), field)], left[...], right[...])
    sent[0] = real.astype(bf16)
    sent[1] = imag.astype(bf16)


def far_kernel(turn, early, start, left, right, frames, wave, arrived, kept, given, last):
    own = own_first()
    side = start.shape[2]
    field = pair(arrived)
    if early:
        (field,) = propagate([field], left[...], right[...])
        outer = multiply(pair(wave), field)
        (field,) = propagate([multiply(pair(frames, 1), field)], left[...], right[...])
    else:
        outer = multiply(pair(wave), field)
        (field,) = propagate([multiply(pair(frames, 1), field)], left[:, side:], right[side:])
    first = multiply(pair(start, turn), field)
    for plane, sign in ((0, 1.0), (1, -1.0)):
        kept[plane] = (jnp.where(own == 0, first[plane], outer[plane]) * sign).astype(bf16)
        given[plane] = (jnp.where(own == 0, outer[plane], first[plane]) * sign).astype(bf16)
    last[0], last[1] = multiply(pair(frames, 0), field)


def part_kernel(home, width, places, *refs):
    count = places.shape[1]
    windows, outs = refs[: 2 * count], refs[2 * count :]
    _, _, _, strip, side = outs[0].shape
    row = lax.broadcasted_iota(jnp.int32, (strip, side), 0)
    for flip in range(2):
        for turn in range(count):
            window = windows[flip * count + turn]
            down, _ = window_place(places, home, turn, strip, width, flip)
            for plane in range(2):
                ends = window[plane, :strip].astype(f32)
                outs[0][flip, turn, plane] = jnp.where(row < down, 0.0, ends).astype(bf16)
                outs[-1][flip, turn, plane] = jnp.where(row < down, ends, 0.0).astype(bf16)
                for step in range(1, len(outs) - 1):
                    outs[step][flip, turn, plane] = window[
                        plane, step * strip : (step + 1) * strip
                    ]


def probe_kernel(home, strip, width, places, *refs):
    waves, (near, away, sent, total) = refs[:-4], refs[-4:]
    core, half = this_place()
    weight = jnp.where(half == 0, 1.0, 0.0)
    for plane, sign in ((0, weight), (1, -weight)):
        parts = []
        for turn, wave in enumerate(waves):
            down, across = window_place(places, home, turn, strip, width)
            parts.append(turned_back(wave[plane], down, across))
        total[plane] = sum(parts) * sign
    height = near.shape[1]
    for index, out in enumerate((near, away)):
        for plane in range(2):
            mine = pl.multiple_of((2 * index + core) * height, height)
            other = pl.multiple_of((2 * index + (core ^ 1)) * height, height)
            out[plane] = total[plane, pl.ds(mine, height)]
            sent[index, plane] = total[plane, pl.ds(other, height)].astype(bf16)


def deposit_kernel(reach, *refs):
    places, pieces, out = refs[:reach], refs[reach:-1], refs[-1]
    _, count, _, strip, side = pieces[0].shape
    width = out.shape[2]
    core, _ = this_place()
    lane = lax.broadcasted_iota(jnp.int32, (strip, LANES), 1)
    out[...] = jnp.zeros(out.shape, f32)
    for step, piece in enumerate(pieces):
        for flip in range(2):
            for turn in range(count):
                column = column_of(places[step], width, core ^ flip, turn)
                base, after, begin = stretch(column, side, width)
                rest = pl.multiple_of(base + LANES, LANES)
                for plane in range(2):
                    ends = piece[flip, turn, plane, :, :LANES].astype(f32)
                    out[plane, :, pl.ds(base, LANES)] += jnp.where(lane < begin, 0.0, ends)
                    out[plane, :, pl.ds(rest, side - LANES)] += piece[
                        flip, turn, plane, :, LANES:
                    ].astype(f32)
                    out[plane, :, pl.ds(after, LANES)] += jnp.where(lane < begin, ends, 0.0)


def local(transmission, probe, exit_adjoint, scan_row, scan_col):
    depth = lax.axis_size("depth")
    regions = lax.axis_size("scan")
    strip, width = transmission.shape[2:]
    side = probe.shape[1]
    reach = side // strip + 1
    home = reach // 2
    count = scan_row.shape[1]
    assert transmission.shape[0] == 1 and depth == 4 and scan_row.shape[0] == 2
    assert side == 2 * LANES and count == 2

    def along_scan(value, by):
        return lax.ppermute(value, "scan", [(i, (i + by) % regions) for i in range(regions)])

    def across(value, flip, by, sections=range(depth)):
        if flip == 0 and by == 0:
            return value
        route = [
            (d * regions + i, (d ^ flip) * regions + (i + by) % regions)
            for d in sections
            for i in range(regions)
        ]
        return lax.ppermute(value, ("depth", "scan"), route)

    smem = pl.BlockSpec(memory_space=pltpu.SMEM)
    vmem = pl.BlockSpec(memory_space=pltpu.VMEM)

    def call(kernel, out_shape, in_specs, flops, name, scratch=(), limit=24):
        return pl.pallas_call(
            kernel,
            out_shape=out_shape,
            in_specs=in_specs,
            out_specs=jax.tree.map(lambda _: vmem, out_shape),
            scratch_shapes=scratch,
            compiler_params=pltpu.CompilerParams(vmem_limit_bytes=limit << 20),
            cost_estimate=pl.CostEstimate(flops=flops, bytes_accessed=4 << 20, transcendentals=0),
            name=name,
        )

    shape = jax.ShapeDtypeStruct
    piece = shape((count, 2, strip, side), bf16)
    wave = (2, side, side)
    field = (count,) + wave
    left, right = (jnp.asarray(table) for table in tables(side))
    lower = range(depth // 2)

    adjoint = call(
        pick_kernel,
        shape(wave, bf16),
        [pl.BlockSpec(memory_space=pltpu.HBM)],
        1 << 20,
        "pick",
        [pltpu.VMEM(wave, f32), pltpu.SemaphoreType.DMA((4,))],
        62,
    )(exit_adjoint)
    adjoint, scan_row = lax.optimization_barrier((adjoint, scan_row))
    adjoint = along_scan(adjoint, home)
    packed = scan_row * width + scan_col
    places = [packed] + [along_scan(packed, step) for step in range(1, reach)]

    order = [(flip, step) for flip in range(2) for step in range(reach)]
    far_first = sorted(order, key=lambda key: -abs(key[1] - home))
    pieces = {}
    for steps in (range(home + 1), range(home + 1, reach)):
        keys = [(flip, step) for flip in range(2) for step in steps]
        cut = call(
            functools.partial(extract_kernel, len(steps)),
            [piece] * len(keys),
            [smem] * len(steps) + [vmem],
            1 << 26,
            "extract",
        )(*(places[step] for step in steps), transmission[0])
        pieces.update(zip(keys, cut))
    adjoint, pieces[0, home] = lax.optimization_barrier((adjoint, pieces[0, home]))
    adjoints = [adjoint, across(adjoint, 2, 0, lower)]
    for flip, step in far_first:
        if (flip, step) == (1, home):
            pieces[1, home], pieces[0, 0] = lax.optimization_barrier((pieces[1, home], pieces[0, 0]))
        pieces[flip, step] = across(pieces[flip, step], flip, home - step)

    start = call(
        functools.partial(start_kernel, home, strip, width),
        shape(field, f32),
        [smem] + [vmem] * (3 + count),
        1 << 30,
        "start",
    )(places[home], probe, *adjoints, left, right)
    chains = []
    for turn in range(count):
        frames, forward, sent = call(
            functools.partial(near_kernel, home, turn, turn == count - 1, width),
            [shape((2,) + wave, bf16), shape(wave, f32), shape(wave, bf16)],
            [smem] + [vmem] * (3 + len(order)),
            1 << 30,
            "near",
        )(places[home], start, left, right, *(pieces[key] for key in order))
        chains.append((frames, forward, across(sent, 2, 0)))
    kept, given, lasts = [], [], []
    for turn, chain in enumerate(chains):
        mine, other, last = call(
            functools.partial(far_kernel, turn, turn == count - 1),
            [shape(wave, bf16)] * 2 + [shape(wave, f32)],
            [vmem] * 6,
            1 << 31,
            "far",
        )(start, left, right, *chain)
        kept.append(mine)
        given.append(across(other, 1, 0))
        lasts.append(last)
    parts = call(
        functools.partial(part_kernel, home, width),
        [shape((2,) + piece.shape, bf16)] * reach,
        [smem] + [vmem] * (2 * count),
        1 << 26,
        "part",
    )(places[home], *kept, *given)
    parts = list(parts)

    height = side // depth
    near, away, probe_sent = call(
        functools.partial(probe_kernel, home, strip, width),
        [shape((2, height, side), f32)] * 2 + [shape((2, 2, height, side), bf16)],
        [smem] + [vmem] * count,
        1 << 26,
        "probe",
        [pltpu.VMEM(wave, f32)],
    )(places[home], *lasts)
    returned = [across(part, 0, step - home) for step, part in enumerate(parts)]

    def scan_round(total, span):
        rounded = total.astype(bf16)
        route = [(i, i ^ span) for i in range(regions)]
        return rounded.astype(f32) + lax.ppermute(rounded, "scan", route).astype(f32)

    def probe_rounds(_, held):
        near, away, given = held
        away = across((away + given[1].astype(f32)).astype(bf16), 2, 0, lower).astype(f32)
        total = jnp.where(half == 0, near + given[0].astype(f32), away)
        for span in spans[:-1]:
            total = scan_round(total, span)
        return total, away, given

    half = lax.axis_index("depth") // (depth // 2)
    once = lax.axis_index("depth") // depth + 1
    assert regions & (regions - 1) == 0
    spans = [1 << level for level in range(regions.bit_length() - 1)]
    near, parts[home] = lax.optimization_barrier((near, parts[home]))
    probe_grad, *_ = lax.fori_loop(
        0, once, probe_rounds, (near, away, across(probe_sent, 1, 0))
    )
    probe_grad, returned = lax.optimization_barrier((probe_grad, returned))
    probe_grad = scan_round(probe_grad, spans[-1])
    object_grad = call(
        functools.partial(deposit_kernel, reach),
        shape(transmission.shape[1:], f32),
        [smem] * reach + [vmem] * reach,
        1 << 26,
        "deposit",
    )(*places, *returned)
    return object_grad[None], probe_grad


def solution(mesh):
    placed = (
        P("depth", None, "scan", None),
        P(),
        P(None, "scan", None, None, None),
        P(None, "scan"),
        P(None, "scan"),
    )
    return jax.shard_map(
        local,
        mesh=mesh,
        in_specs=placed,
        out_specs=(P("depth", None, "scan", None), P(None, "depth", None)),
        check_vma=False,
    )
```

```python
import functools

import jax
import jax.numpy as jnp
import numpy as np
from jax import lax
from jax.experimental import pallas as pl
from jax.experimental.pallas import tpu as pltpu
from jax.sharding import PartitionSpec as P

fresnel = 0.25
LANES = 128
bf16 = jnp.bfloat16
f32 = jnp.float32


def propagator(extent):
    indices = np.arange(extent)
    frequency = np.where(indices < extent // 2, indices, indices - extent).astype(np.float64)
    factor = np.exp(-1j * np.pi * fresnel / extent * frequency * frequency)
    column = np.fft.ifft(factor)
    matrix = column[(indices[:, None] - indices[None, :]) % extent]
    return matrix.real, matrix.imag


def halves(matrix):
    high = matrix.astype(np.float32).astype(bf16)
    low = (matrix - high.astype(np.float64)).astype(np.float32).astype(bf16)
    return high, low


def tables(extent):
    real, imag = propagator(extent)
    left = halves(np.concatenate([real, imag], axis=0))
    right = halves(np.concatenate([real, imag], axis=1))
    left_table = np.concatenate([left[0], left[0], left[1]], axis=1)
    right_table = np.concatenate([right[0], right[0], right[1]], axis=0)
    return left_table, right_table


def split(values):
    high = values.astype(bf16)
    low = (values - high.astype(f32)).astype(bf16)
    return high, low


def propagate(fields, left, right):
    side = fields[0][0].shape[0]

    def parts(values, axis):
        high, low = split(values)
        if left.shape[1] == 3 * side:
            return jnp.concatenate([high, low, high], axis=axis)
        return jnp.concatenate([high, high], axis=axis)

    columns = parts(jnp.concatenate([part for field in fields for part in field], axis=1), 0)
    middle = jnp.dot(left, columns, preferred_element_type=f32)
    rows = []
    for index in range(len(fields)):
        by_real = middle[:side, 2 * index * side : 2 * (index + 1) * side]
        by_imag = middle[side:, 2 * index * side : 2 * (index + 1) * side]
        rows.append(by_real[:, :side] - by_imag[:, side:])
        rows.append(by_real[:, side:] + by_imag[:, :side])
    result = jnp.dot(parts(jnp.concatenate(rows, axis=0), 1), right, preferred_element_type=f32)
    results = []
    for index in range(len(fields)):
        real = result[2 * index * side : (2 * index + 1) * side]
        imag = result[(2 * index + 1) * side : 2 * (index + 1) * side]
        results.append((real[:, :side] - imag[:, side:], real[:, side:] + imag[:, :side]))
    return results


def multiply(first, second):
    return (
        first[0] * second[0] - first[1] * second[1],
        first[0] * second[1] + first[1] * second[0],
    )


def turned(values, down, across):
    return pltpu.roll(pltpu.roll(values, down, 0), across, 1)


def turned_back(values, down, across):
    rows, columns = values.shape
    return turned(values, lax.rem(rows - down, rows), lax.rem(columns - across, columns))


def stretch(column, side, width):
    base = pl.multiple_of(column // LANES * LANES, LANES)
    after = pl.multiple_of(jnp.minimum(base + side, width - LANES), LANES)
    return base, after, column - base


def this_place():
    section = lax.axis_index("depth")
    return section % 2, section // 2


def column_of(places, width, *index):
    return lax.rem(places[index], width)


def window_place(places, home, turn, strip, width, flip=0):
    core, _ = this_place()
    regions = lax.axis_size("scan")
    source = lax.rem(lax.axis_index("scan") - home + regions, regions)
    value = places[core ^ flip, turn]
    return value // width - source * strip, lax.rem(lax.rem(value, width), LANES)


def pick_kernel(waves, out, buffer, arrived):
    core, half = this_place()
    copy = pltpu.make_async_copy(waves.at[core, 1 - half], buffer, arrived)
    copy.start()
    copy.wait()
    out[...] = buffer[...].astype(bf16)


def extract_kernel(reach, *refs):
    places, (strip, *outs) = refs[:reach], refs[reach:]
    count, _, rows, side = outs[0].shape
    width = strip.shape[2]
    core, _ = this_place()
    lane = lax.broadcasted_iota(jnp.int32, (rows, LANES), 1)
    for flip in range(2):
        for step in range(reach):
            out = outs[flip * reach + step]
            for turn in range(count):
                column = column_of(places[step], width, core ^ flip, turn)
                base, after, begin = stretch(column, side, width)
                rest = pl.multiple_of(base + LANES, LANES)
                for plane in range(2):
                    first = strip[plane, :, pl.ds(base, LANES)]
                    again = strip[plane, :, pl.ds(after, LANES)]
                    out[turn, plane, :, :LANES] = jnp.where(lane < begin, again, first).astype(bf16)
                    out[turn, plane, :, LANES:] = strip[plane, :, pl.ds(rest, side - LANES)].astype(
                        bf16
                    )


def start_kernel(home, strip, width, places, probe, *refs):
    adjoints, (left, right, out) = refs[:-3], refs[-3:]
    _, half = this_place()

    @pl.when(half == 0)
    def _():
        for turn in range(len(adjoints)):
            down, across = window_place(places, home, turn, strip, width)
            for plane in range(2):
                out[turn, plane] = turned(probe[plane], down, across)

    @pl.when(half != 0)
    def _():
        fields = []
        for turn, adjoint in enumerate(adjoints):
            down, across = window_place(places, home, turn, strip, width)
            real, imag = (turned(adjoint[plane].astype(f32), down, across) for plane in range(2))
            fields.append((real, -imag))
        for turn, field in enumerate(propagate(fields, left[...], right[...])):
            out[turn, 0], out[turn, 1] = field


def pair(ref, *index):
    return ref[(*index, 0)].astype(f32), ref[(*index, 1)].astype(f32)


def own_first():
    core, half = this_place()
    return jnp.where(core == half, 0, 1)


def near_kernel(home, turn, early, width, places, start, left, right, *refs):
    pieces, (frames, wave, sent) = refs[:-3], refs[-3:]
    reach = len(pieces) // 2
    _, _, strip, side = pieces[0].shape
    own = own_first()
    row = lax.broadcasted_iota(jnp.int32, (strip, side), 0)
    down, _ = window_place(places, home, turn, strip, width)
    for flip in range(2):
        parts = pieces[flip * reach : (flip + 1) * reach]
        for plane in range(2):
            first = parts[0][turn, plane].astype(f32)
            again = parts[-1][turn, plane].astype(f32)
            frames[own ^ flip, plane, :strip] = jnp.where(row < down, again, first).astype(bf16)
            for step in range(1, reach - 1):
                frames[own ^ flip, plane, step * strip : (step + 1) * strip] = parts[step][
                    turn, plane
                ]
    field = multiply(pair(frames, 0), pair(start, turn))
    if early:
        (field,) = propagate([field], left[:, side:], right[side:])
        wave[0], wave[1] = field
        real, imag = multiply(pair(frames, 1), field)
    else:
        (field,) = propagate([field], left[...], right[...])
        wave[0], wave[1] = field
        ((real, imag),) = propagate([multiply(pair(frames, 1), field)], left[...], right[...])
    sent[0] = real.astype(bf16)
    sent[1] = imag.astype(bf16)


def far_kernel(turn, early, start, left, right, frames, wave, arrived, kept, given, last):
    own = own_first()
    side = start.shape[2]
    field = pair(arrived)
    if early:
        (field,) = propagate([field], left[...], right[...])
        outer = multiply(pair(wave), field)
        (field,) = propagate([multiply(pair(frames, 1), field)], left[...], right[...])
    else:
        outer = multiply(pair(wave), field)
        (field,) = propagate([multiply(pair(frames, 1), field)], left[:, side:], right[side:])
    first = multiply(pair(start, turn), field)
    for plane, sign in ((0, 1.0), (1, -1.0)):
        kept[plane] = (jnp.where(own == 0, first[plane], outer[plane]) * sign).astype(bf16)
        given[plane] = (jnp.where(own == 0, outer[plane], first[plane]) * sign).astype(bf16)
    last[0], last[1] = multiply(pair(frames, 0), field)


def part_kernel(home, width, places, *refs):
    count = places.shape[1]
    windows, outs = refs[: 2 * count], refs[2 * count :]
    _, _, _, strip, side = outs[0].shape
    row = lax.broadcasted_iota(jnp.int32, (strip, side), 0)
    for flip in range(2):
        for turn in range(count):
            window = windows[flip * count + turn]
            down, _ = window_place(places, home, turn, strip, width, flip)
            for plane in range(2):
                ends = window[plane, :strip].astype(f32)
                outs[0][flip, turn, plane] = jnp.where(row < down, 0.0, ends).astype(bf16)
                outs[-1][flip, turn, plane] = jnp.where(row < down, ends, 0.0).astype(bf16)
                for step in range(1, len(outs) - 1):
                    outs[step][flip, turn, plane] = window[
                        plane, step * strip : (step + 1) * strip
                    ]


def probe_kernel(home, strip, width, places, *refs):
    waves, (near, away, sent, total) = refs[:-4], refs[-4:]
    core, half = this_place()
    weight = jnp.where(half == 0, 1.0, 0.0)
    for plane, sign in ((0, weight), (1, -weight)):
        parts = []
        for turn, wave in enumerate(waves):
            down, across = window_place(places, home, turn, strip, width)
            parts.append(turned_back(wave[plane], down, across))
        total[plane] = sum(parts) * sign
    height = near.shape[1]
    for index, out in enumerate((near, away)):
        for plane in range(2):
            mine = pl.multiple_of((2 * index + core) * height, height)
            other = pl.multiple_of((2 * index + (core ^ 1)) * height, height)
            out[plane] = total[plane, pl.ds(mine, height)]
            sent[index, plane] = total[plane, pl.ds(other, height)].astype(bf16)


def deposit_kernel(steps, *refs):
    reach = len(steps)
    places, pieces, out = refs[:reach], refs[reach:-1], refs[-1]
    _, count, _, strip, side = pieces[0].shape
    width = out.shape[2]
    core, _ = this_place()
    lane = lax.broadcasted_iota(jnp.int32, (strip, LANES), 1)
    out[...] = jnp.zeros(out.shape, f32)
    for step, piece in zip(steps, pieces):
        for flip in range(2):
            for turn in range(count):
                column = column_of(places[step], width, core ^ flip, turn)
                base, after, begin = stretch(column, side, width)
                rest = pl.multiple_of(base + LANES, LANES)
                for plane in range(2):
                    ends = piece[flip, turn, plane, :, :LANES].astype(f32)
                    out[plane, :, pl.ds(base, LANES)] += jnp.where(lane < begin, 0.0, ends)
                    out[plane, :, pl.ds(rest, side - LANES)] += piece[
                        flip, turn, plane, :, LANES:
                    ].astype(f32)
                    out[plane, :, pl.ds(after, LANES)] += jnp.where(lane < begin, ends, 0.0)


def local(transmission, probe, exit_adjoint, scan_row, scan_col):
    depth = lax.axis_size("depth")
    regions = lax.axis_size("scan")
    strip, width = transmission.shape[2:]
    side = probe.shape[1]
    reach = side // strip + 1
    home = reach // 2
    count = scan_row.shape[1]
    assert transmission.shape[0] == 1 and depth == 4 and scan_row.shape[0] == 2
    assert side == 2 * LANES and count == 2

    def along_scan(value, by):
        return lax.ppermute(value, "scan", [(i, (i + by) % regions) for i in range(regions)])

    def across(value, flip, by, sections=range(depth)):
        if flip == 0 and by == 0:
            return value
        route = [
            (d * regions + i, (d ^ flip) * regions + (i + by) % regions)
            for d in sections
            for i in range(regions)
        ]
        return lax.ppermute(value, ("depth", "scan"), route)

    smem = pl.BlockSpec(memory_space=pltpu.SMEM)
    vmem = pl.BlockSpec(memory_space=pltpu.VMEM)

    def call(kernel, out_shape, in_specs, flops, name, scratch=(), limit=24):
        return pl.pallas_call(
            kernel,
            out_shape=out_shape,
            in_specs=in_specs,
            out_specs=jax.tree.map(lambda _: vmem, out_shape),
            scratch_shapes=scratch,
            compiler_params=pltpu.CompilerParams(vmem_limit_bytes=limit << 20),
            cost_estimate=pl.CostEstimate(flops=flops, bytes_accessed=4 << 20, transcendentals=0),
            name=name,
        )

    shape = jax.ShapeDtypeStruct
    piece = shape((count, 2, strip, side), bf16)
    wave = (2, side, side)
    field = (count,) + wave
    left, right = (jnp.asarray(table) for table in tables(side))
    lower = range(depth // 2)

    adjoint = call(
        pick_kernel,
        shape(wave, bf16),
        [pl.BlockSpec(memory_space=pltpu.HBM)],
        1 << 20,
        "pick",
        [pltpu.VMEM(wave, f32), pltpu.SemaphoreType.DMA],
        62,
    )(exit_adjoint)
    adjoint, scan_row = lax.optimization_barrier((adjoint, scan_row))
    adjoint = along_scan(adjoint, home)
    packed = scan_row * width + scan_col
    places = [packed] + [along_scan(packed, step) for step in range(1, reach)]

    order = [(flip, step) for flip in range(2) for step in range(reach)]
    far_first = sorted(order, key=lambda key: -abs(key[1] - home))
    pieces = call(
        functools.partial(extract_kernel, reach),
        [piece] * len(order),
        [smem] * reach + [vmem],
        1 << 26,
        "extract",
    )(*places, transmission[0])
    pieces = dict(zip(order, pieces))
    adjoint, pieces[0, home] = lax.optimization_barrier((adjoint, pieces[0, home]))
    adjoints = [adjoint, across(adjoint, 2, 0, lower)]
    for flip, step in far_first:
        if (flip, step) == (1, home):
            pieces[1, home], pieces[0, 0] = lax.optimization_barrier((pieces[1, home], pieces[0, 0]))
        pieces[flip, step] = across(pieces[flip, step], flip, home - step)

    start = call(
        functools.partial(start_kernel, home, strip, width),
        shape(field, f32),
        [smem] + [vmem] * (3 + count),
        1 << 30,
        "start",
    )(places[home], probe, *adjoints, left, right)
    chains = []
    for turn in range(count):
        frames, forward, sent = call(
            functools.partial(near_kernel, home, turn, turn == count - 1, width),
            [shape((2,) + wave, bf16), shape(wave, f32), shape(wave, bf16)],
            [smem] + [vmem] * (3 + len(order)),
            1 << 30,
            "near",
        )(places[home], start, left, right, *(pieces[key] for key in order))
        chains.append((frames, forward, across(sent, 2, 0)))
    kept, given, lasts = [], [], []
    for turn, chain in enumerate(chains):
        mine, other, last = call(
            functools.partial(far_kernel, turn, turn == count - 1),
            [shape(wave, bf16)] * 2 + [shape(wave, f32)],
            [vmem] * 6,
            1 << 31,
            "far",
        )(start, left, right, *chain)
        kept.append(mine)
        given.append(across(other, 1, 0))
        lasts.append(last)
    parts = call(
        functools.partial(part_kernel, home, width),
        [shape((2,) + piece.shape, bf16)] * reach,
        [smem] + [vmem] * (2 * count),
        1 << 26,
        "part",
    )(places[home], *kept, *given)
    parts = list(parts)

    height = side // depth
    near, away, probe_sent = call(
        functools.partial(probe_kernel, home, strip, width),
        [shape((2, height, side), f32)] * 2 + [shape((2, 2, height, side), bf16)],
        [smem] + [vmem] * count,
        1 << 26,
        "probe",
        [pltpu.VMEM(wave, f32)],
    )(places[home], *lasts)
    returned = [across(part, 0, step - home) for step, part in enumerate(parts)]

    def scan_round(total, span):
        rounded = total.astype(bf16)
        route = [(i, i ^ span) for i in range(regions)]
        return rounded.astype(f32) + lax.ppermute(rounded, "scan", route).astype(f32)

    def probe_rounds(_, held):
        near, away, given = held
        away = across((away + given[1].astype(f32)).astype(bf16), 2, 0, lower).astype(f32)
        total = jnp.where(half == 0, near + given[0].astype(f32), away)
        for span in spans[:-1]:
            total = scan_round(total, span)
        return total, away, given

    half = lax.axis_index("depth") // (depth // 2)
    once = lax.axis_index("depth") // depth + 1
    assert regions & (regions - 1) == 0
    spans = [1 << level for level in range(regions.bit_length() - 1)]
    spans = spans[-1:] + spans[:-1]
    near, parts[home] = lax.optimization_barrier((near, parts[home]))
    probe_grad, *_ = lax.fori_loop(
        0, once, probe_rounds, (near, away, across(probe_sent, 1, 0))
    )
    probe_grad, returned = lax.optimization_barrier((probe_grad, returned))
    probe_grad = scan_round(probe_grad, spans[-1])
    far_steps = sorted(range(reach), key=lambda step: -abs(step - home))
    object_grad = call(
        functools.partial(deposit_kernel, far_steps),
        shape(transmission.shape[1:], f32),
        [smem] * reach + [vmem] * reach,
        1 << 26,
        "deposit",
    )(*places, *(returned[step] for step in far_steps))
    return object_grad[None], probe_grad


def solution(mesh):
    placed = (
        P("depth", None, "scan", None),
        P(),
        P(None, "scan", None, None, None),
        P(None, "scan"),
        P(None, "scan"),
    )
    return jax.shard_map(
        local,
        mesh=mesh,
        in_specs=placed,
        out_specs=(P("depth", None, "scan", None), P(None, "depth", None)),
        check_vma=False,
    )
```

```python
import functools

import jax
import jax.numpy as jnp
import numpy as np
from jax import lax
from jax.experimental import pallas as pl
from jax.experimental.pallas import tpu as pltpu
from jax.sharding import PartitionSpec as P

fresnel = 0.25
LANES = 128
bf16 = jnp.bfloat16
f32 = jnp.float32


def propagator(extent):
    indices = np.arange(extent)
    frequency = np.where(indices < extent // 2, indices, indices - extent).astype(np.float64)
    factor = np.exp(-1j * np.pi * fresnel / extent * frequency * frequency)
    column = np.fft.ifft(factor)
    matrix = column[(indices[:, None] - indices[None, :]) % extent]
    return matrix.real, matrix.imag


def halves(matrix):
    high = matrix.astype(np.float32).astype(bf16)
    low = (matrix - high.astype(np.float64)).astype(np.float32).astype(bf16)
    return high, low


def tables(extent):
    real, imag = propagator(extent)
    left = halves(np.concatenate([real, imag], axis=0))
    right = halves(np.concatenate([real, imag], axis=1))
    left_table = np.concatenate([left[0], left[0], left[1]], axis=1)
    right_table = np.concatenate([right[0], right[0], right[1]], axis=0)
    return left_table, right_table


def split(values):
    high = values.astype(bf16)
    low = (values - high.astype(f32)).astype(bf16)
    return high, low


def propagate(fields, left, right):
    side = fields[0][0].shape[0]

    def parts(values, axis):
        high, low = split(values)
        if left.shape[1] == 3 * side:
            return jnp.concatenate([high, low, high], axis=axis)
        return jnp.concatenate([high, high], axis=axis)

    columns = parts(jnp.concatenate([part for field in fields for part in field], axis=1), 0)
    middle = jnp.dot(left, columns, preferred_element_type=f32)
    rows = []
    for index in range(len(fields)):
        by_real = middle[:side, 2 * index * side : 2 * (index + 1) * side]
        by_imag = middle[side:, 2 * index * side : 2 * (index + 1) * side]
        rows.append(by_real[:, :side] - by_imag[:, side:])
        rows.append(by_real[:, side:] + by_imag[:, :side])
    result = jnp.dot(parts(jnp.concatenate(rows, axis=0), 1), right, preferred_element_type=f32)
    results = []
    for index in range(len(fields)):
        real = result[2 * index * side : (2 * index + 1) * side]
        imag = result[(2 * index + 1) * side : 2 * (index + 1) * side]
        results.append((real[:, :side] - imag[:, side:], real[:, side:] + imag[:, :side]))
    return results


def multiply(first, second):
    return (
        first[0] * second[0] - first[1] * second[1],
        first[0] * second[1] + first[1] * second[0],
    )


def turned(values, down, across):
    return pltpu.roll(pltpu.roll(values, down, 0), across, 1)


def turned_back(values, down, across):
    rows, columns = values.shape
    return turned(values, lax.rem(rows - down, rows), lax.rem(columns - across, columns))


def stretch(column, side, width):
    base = pl.multiple_of(column // LANES * LANES, LANES)
    after = pl.multiple_of(jnp.minimum(base + side, width - LANES), LANES)
    return base, after, column - base


def this_place():
    section = lax.axis_index("depth")
    return section % 2, section // 2


def column_of(places, width, *index):
    return lax.rem(places[index], width)


def window_place(places, home, turn, strip, width, flip=0):
    core, _ = this_place()
    regions = lax.axis_size("scan")
    source = lax.rem(lax.axis_index("scan") - home + regions, regions)
    value = places[core ^ flip, turn]
    return value // width - source * strip, lax.rem(lax.rem(value, width), LANES)


def pick_kernel(waves, out, buffer, arrived):
    core, half = this_place()
    copy = pltpu.make_async_copy(waves.at[core, 1 - half], buffer, arrived)
    copy.start()
    copy.wait()
    out[...] = buffer[...].astype(bf16)


def extract_kernel(reach, *refs):
    places, (strip, *outs) = refs[:reach], refs[reach:]
    count, _, rows, side = outs[0].shape
    width = strip.shape[2]
    core, _ = this_place()
    lane = lax.broadcasted_iota(jnp.int32, (rows, LANES), 1)
    for flip in range(2):
        for step in range(reach):
            out = outs[flip * reach + step]
            for turn in range(count):
                column = column_of(places[step], width, core ^ flip, turn)
                base, after, begin = stretch(column, side, width)
                rest = pl.multiple_of(base + LANES, LANES)
                for plane in range(2):
                    first = strip[plane, :, pl.ds(base, LANES)]
                    again = strip[plane, :, pl.ds(after, LANES)]
                    out[turn, plane, :, :LANES] = jnp.where(lane < begin, again, first).astype(bf16)
                    out[turn, plane, :, LANES:] = strip[plane, :, pl.ds(rest, side - LANES)].astype(
                        bf16
                    )


def start_kernel(home, strip, width, places, probe, *refs):
    adjoints, (left, right, out) = refs[:-3], refs[-3:]
    _, half = this_place()

    @pl.when(half == 0)
    def _():
        for turn in range(len(adjoints)):
            down, across = window_place(places, home, turn, strip, width)
            for plane in range(2):
                out[turn, plane] = turned(probe[plane], down, across)

    @pl.when(half != 0)
    def _():
        fields = []
        for turn, adjoint in enumerate(adjoints):
            down, across = window_place(places, home, turn, strip, width)
            real, imag = (turned(adjoint[plane].astype(f32), down, across) for plane in range(2))
            fields.append((real, -imag))
        for turn, field in enumerate(propagate(fields, left[...], right[...])):
            out[turn, 0], out[turn, 1] = field


def pair(ref, *index):
    return ref[(*index, 0)].astype(f32), ref[(*index, 1)].astype(f32)


def own_first():
    core, half = this_place()
    return jnp.where(core == half, 0, 1)


def near_kernel(home, turn, early, width, places, start, left, right, *refs):
    pieces, (frames, wave, sent) = refs[:-3], refs[-3:]
    reach = len(pieces) // 2
    _, _, strip, side = pieces[0].shape
    own = own_first()
    row = lax.broadcasted_iota(jnp.int32, (strip, side), 0)
    down, _ = window_place(places, home, turn, strip, width)
    for flip in range(2):
        parts = pieces[flip * reach : (flip + 1) * reach]
        for plane in range(2):
            first = parts[0][turn, plane].astype(f32)
            again = parts[-1][turn, plane].astype(f32)
            frames[own ^ flip, plane, :strip] = jnp.where(row < down, again, first).astype(bf16)
            for step in range(1, reach - 1):
                frames[own ^ flip, plane, step * strip : (step + 1) * strip] = parts[step][
                    turn, plane
                ]
    field = multiply(pair(frames, 0), pair(start, turn))
    if early:
        (field,) = propagate([field], left[:, side:], right[side:])
        wave[0], wave[1] = field
        real, imag = multiply(pair(frames, 1), field)
    else:
        (field,) = propagate([field], left[...], right[...])
        wave[0], wave[1] = field
        ((real, imag),) = propagate([multiply(pair(frames, 1), field)], left[...], right[...])
    sent[0] = real.astype(bf16)
    sent[1] = imag.astype(bf16)


def far_kernel(turn, early, start, left, right, frames, wave, arrived, kept, given, last):
    own = own_first()
    side = start.shape[2]
    field = pair(arrived)
    if early:
        (field,) = propagate([field], left[...], right[...])
        outer = multiply(pair(wave), field)
        (field,) = propagate([multiply(pair(frames, 1), field)], left[...], right[...])
    else:
        outer = multiply(pair(wave), field)
        (field,) = propagate([multiply(pair(frames, 1), field)], left[:, side:], right[side:])
    first = multiply(pair(start, turn), field)
    for plane, sign in ((0, 1.0), (1, -1.0)):
        kept[plane] = (jnp.where(own == 0, first[plane], outer[plane]) * sign).astype(bf16)
        given[plane] = (jnp.where(own == 0, outer[plane], first[plane]) * sign).astype(bf16)
    last[0], last[1] = multiply(pair(frames, 0), field)


def part_kernel(home, width, places, *refs):
    count = places.shape[1]
    windows, outs = refs[: 2 * count], refs[2 * count :]
    _, _, _, strip, side = outs[0].shape
    row = lax.broadcasted_iota(jnp.int32, (strip, side), 0)
    for flip in range(2):
        for turn in range(count):
            window = windows[flip * count + turn]
            down, _ = window_place(places, home, turn, strip, width, flip)
            for plane in range(2):
                ends = window[plane, :strip].astype(f32)
                outs[0][flip, turn, plane] = jnp.where(row < down, 0.0, ends).astype(bf16)
                outs[-1][flip, turn, plane] = jnp.where(row < down, ends, 0.0).astype(bf16)
                for step in range(1, len(outs) - 1):
                    outs[step][flip, turn, plane] = window[
                        plane, step * strip : (step + 1) * strip
                    ]


def probe_kernel(home, strip, width, places, *refs):
    waves, (near, away, sent, total) = refs[:-4], refs[-4:]
    core, half = this_place()
    weight = jnp.where(half == 0, 1.0, 0.0)
    for plane, sign in ((0, weight), (1, -weight)):
        parts = []
        for turn, wave in enumerate(waves):
            down, across = window_place(places, home, turn, strip, width)
            parts.append(turned_back(wave[plane], down, across))
        total[plane] = sum(parts) * sign
    height = near.shape[1]
    for index, out in enumerate((near, away)):
        for plane in range(2):
            mine = pl.multiple_of((2 * index + core) * height, height)
            other = pl.multiple_of((2 * index + (core ^ 1)) * height, height)
            out[plane] = total[plane, pl.ds(mine, height)]
            sent[index, plane] = total[plane, pl.ds(other, height)].astype(bf16)


def deposit_kernel(reach, *refs):
    places, pieces, out = refs[:reach], refs[reach:-1], refs[-1]
    _, count, _, strip, side = pieces[0].shape
    width = out.shape[2]
    core, _ = this_place()
    lane = lax.broadcasted_iota(jnp.int32, (strip, LANES), 1)
    out[...] = jnp.zeros(out.shape, f32)
    for step, piece in enumerate(pieces):
        for flip in range(2):
            for turn in range(count):
                column = column_of(places[step], width, core ^ flip, turn)
                base, after, begin = stretch(column, side, width)
                rest = pl.multiple_of(base + LANES, LANES)
                for plane in range(2):
                    ends = piece[flip, turn, plane, :, :LANES].astype(f32)
                    out[plane, :, pl.ds(base, LANES)] += jnp.where(lane < begin, 0.0, ends)
                    out[plane, :, pl.ds(rest, side - LANES)] += piece[
                        flip, turn, plane, :, LANES:
                    ].astype(f32)
                    out[plane, :, pl.ds(after, LANES)] += jnp.where(lane < begin, ends, 0.0)


def local(transmission, probe, exit_adjoint, scan_row, scan_col):
    depth = lax.axis_size("depth")
    regions = lax.axis_size("scan")
    strip, width = transmission.shape[2:]
    side = probe.shape[1]
    reach = side // strip + 1
    home = reach // 2
    count = scan_row.shape[1]
    assert transmission.shape[0] == 1 and depth == 4 and scan_row.shape[0] == 2
    assert side == 2 * LANES and count == 2

    def along_scan(value, by):
        return lax.ppermute(value, "scan", [(i, (i + by) % regions) for i in range(regions)])

    def across(value, flip, by, sections=range(depth)):
        if flip == 0 and by == 0:
            return value
        route = [
            (d * regions + i, (d ^ flip) * regions + (i + by) % regions)
            for d in sections
            for i in range(regions)
        ]
        return lax.ppermute(value, ("depth", "scan"), route)

    smem = pl.BlockSpec(memory_space=pltpu.SMEM)
    vmem = pl.BlockSpec(memory_space=pltpu.VMEM)

    def call(kernel, out_shape, in_specs, flops, name, scratch=(), limit=24):
        return pl.pallas_call(
            kernel,
            out_shape=out_shape,
            in_specs=in_specs,
            out_specs=jax.tree.map(lambda _: vmem, out_shape),
            scratch_shapes=scratch,
            compiler_params=pltpu.CompilerParams(vmem_limit_bytes=limit << 20),
            cost_estimate=pl.CostEstimate(flops=flops, bytes_accessed=4 << 20, transcendentals=0),
            name=name,
        )

    shape = jax.ShapeDtypeStruct
    piece = shape((count, 2, strip, side), bf16)
    wave = (2, side, side)
    field = (count,) + wave
    left, right = (jnp.asarray(table) for table in tables(side))
    lower = range(depth // 2)

    adjoint = call(
        pick_kernel,
        shape(wave, bf16),
        [pl.BlockSpec(memory_space=pltpu.HBM)],
        1 << 20,
        "pick",
        [pltpu.VMEM(wave, f32), pltpu.SemaphoreType.DMA],
        62,
    )(exit_adjoint)
    adjoint, scan_row = lax.optimization_barrier((adjoint, scan_row))
    adjoint = along_scan(adjoint, home)
    packed = scan_row * width + scan_col
    places = [packed] + [along_scan(packed, step) for step in range(1, reach)]

    order = [(flip, step) for flip in range(2) for step in range(reach)]
    far_first = sorted(order, key=lambda key: -abs(key[1] - home))
    pieces = call(
        functools.partial(extract_kernel, reach),
        [piece] * len(order),
        [smem] * reach + [vmem],
        1 << 26,
        "extract",
    )(*places, transmission[0])
    pieces = dict(zip(order, pieces))
    adjoint, pieces[0, home] = lax.optimization_barrier((adjoint, pieces[0, home]))
    adjoints = [adjoint, across(adjoint, 2, 0, lower)]
    for flip, step in far_first:
        if (flip, step) == (1, home):
            pieces[1, home], pieces[0, 0] = lax.optimization_barrier((pieces[1, home], pieces[0, 0]))
        pieces[flip, step] = across(pieces[flip, step], flip, home - step)

    start = call(
        functools.partial(start_kernel, home, strip, width),
        shape(field, f32),
        [smem] + [vmem] * (3 + count),
        1 << 30,
        "start",
    )(places[home], probe, *adjoints, left, right)
    chains = []
    for turn in range(count):
        frames, forward, sent = call(
            functools.partial(near_kernel, home, turn, turn == count - 1, width),
            [shape((2,) + wave, bf16), shape(wave, f32), shape(wave, bf16)],
            [smem] + [vmem] * (3 + len(order)),
            1 << 30,
            "near",
        )(places[home], start, left, right, *(pieces[key] for key in order))
        chains.append((frames, forward, across(sent, 2, 0)))
    kept, given, lasts = [], [], []
    for turn, chain in enumerate(chains):
        mine, other, last = call(
            functools.partial(far_kernel, turn, turn == count - 1),
            [shape(wave, bf16)] * 2 + [shape(wave, f32)],
            [vmem] * 6,
            1 << 31,
            "far",
        )(start, left, right, *chain)
        kept.append(mine)
        given.append(across(other, 1, 0))
        lasts.append(last)
    parts = call(
        functools.partial(part_kernel, home, width),
        [shape((2,) + piece.shape, bf16)] * reach,
        [smem] + [vmem] * (2 * count),
        1 << 26,
        "part",
    )(places[home], *kept, *given)
    parts = list(parts)

    height = side // depth
    near, away, probe_sent = call(
        functools.partial(probe_kernel, home, strip, width),
        [shape((2, height, side), f32)] * 2 + [shape((2, 2, height, side), bf16)],
        [smem] + [vmem] * count,
        1 << 26,
        "probe",
        [pltpu.VMEM(wave, f32)],
    )(places[home], *lasts)
    returned = [across(part, 0, step - home) for step, part in enumerate(parts)]

    def scan_round(total, span):
        rounded = total.astype(bf16)
        route = [(i, i ^ span) for i in range(regions)]
        return rounded.astype(f32) + lax.ppermute(rounded, "scan", route).astype(f32)

    def probe_rounds(_, held):
        near, away, given = held
        away = across((away + given[1].astype(f32)).astype(bf16), 2, 0, lower).astype(f32)
        total = jnp.where(half == 0, near + given[0].astype(f32), away)
        for span in spans[:-2]:
            total = scan_round(total, span)
        return total, away, given

    half = lax.axis_index("depth") // (depth // 2)
    once = lax.axis_index("depth") // depth + 1
    assert regions & (regions - 1) == 0
    spans = [1 << level for level in range(regions.bit_length() - 1)]
    near, parts[home] = lax.optimization_barrier((near, parts[home]))
    probe_grad, *_ = lax.fori_loop(
        0, once, probe_rounds, (near, away, across(probe_sent, 1, 0))
    )
    probe_grad, returned = lax.optimization_barrier((probe_grad, returned))
    probe_grad = scan_round(probe_grad, spans[-2])
    object_grad = call(
        functools.partial(deposit_kernel, reach),
        shape(transmission.shape[1:], f32),
        [smem] * reach + [vmem] * reach,
        1 << 26,
        "deposit",
    )(*places, *returned)
    probe_grad, object_grad = lax.optimization_barrier((probe_grad, object_grad))
    probe_grad = scan_round(probe_grad, spans[-1])
    return object_grad[None], probe_grad


def solution(mesh):
    placed = (
        P("depth", None, "scan", None),
        P(),
        P(None, "scan", None, None, None),
        P(None, "scan"),
        P(None, "scan"),
    )
    return jax.shard_map(
        local,
        mesh=mesh,
        in_specs=placed,
        out_specs=(P("depth", None, "scan", None), P(None, "depth", None)),
        check_vma=False,
    )
```

```python
import functools

import jax
import jax.numpy as jnp
import numpy as np
from jax import lax
from jax.experimental import pallas as pl
from jax.experimental.pallas import tpu as pltpu
from jax.sharding import PartitionSpec as P

fresnel = 0.25
LANES = 128
bf16 = jnp.bfloat16
f32 = jnp.float32


def propagator(extent):
    indices = np.arange(extent)
    frequency = np.where(indices < extent // 2, indices, indices - extent).astype(np.float64)
    factor = np.exp(-1j * np.pi * fresnel / extent * frequency * frequency)
    column = np.fft.ifft(factor)
    matrix = column[(indices[:, None] - indices[None, :]) % extent]
    return matrix.real, matrix.imag


def halves(matrix):
    high = matrix.astype(np.float32).astype(bf16)
    low = (matrix - high.astype(np.float64)).astype(np.float32).astype(bf16)
    return high, low


def tables(extent):
    real, imag = propagator(extent)
    left = halves(np.concatenate([real, imag], axis=0))
    right = halves(np.concatenate([real, imag], axis=1))
    left_table = np.concatenate([left[0], left[0], left[1]], axis=1)
    right_table = np.concatenate([right[0], right[0], right[1]], axis=0)
    return left_table, right_table


def split(values):
    high = values.astype(bf16)
    low = (values - high.astype(f32)).astype(bf16)
    return high, low


def propagate(fields, left, right):
    side = fields[0][0].shape[0]

    def parts(values, axis):
        high, low = split(values)
        if left.shape[1] == 3 * side:
            return jnp.concatenate([high, low, high], axis=axis)
        return jnp.concatenate([high, high], axis=axis)

    columns = parts(jnp.concatenate([part for field in fields for part in field], axis=1), 0)
    middle = jnp.dot(left, columns, preferred_element_type=f32)
    rows = []
    for index in range(len(fields)):
        by_real = middle[:side, 2 * index * side : 2 * (index + 1) * side]
        by_imag = middle[side:, 2 * index * side : 2 * (index + 1) * side]
        rows.append(by_real[:, :side] - by_imag[:, side:])
        rows.append(by_real[:, side:] + by_imag[:, :side])
    result = jnp.dot(parts(jnp.concatenate(rows, axis=0), 1), right, preferred_element_type=f32)
    results = []
    for index in range(len(fields)):
        real = result[2 * index * side : (2 * index + 1) * side]
        imag = result[(2 * index + 1) * side : 2 * (index + 1) * side]
        results.append((real[:, :side] - imag[:, side:], real[:, side:] + imag[:, :side]))
    return results


def multiply(first, second):
    return (
        first[0] * second[0] - first[1] * second[1],
        first[0] * second[1] + first[1] * second[0],
    )


def turned(values, down, across):
    return pltpu.roll(pltpu.roll(values, down, 0), across, 1)


def turned_back(values, down, across):
    rows, columns = values.shape
    return turned(values, lax.rem(rows - down, rows), lax.rem(columns - across, columns))


def stretch(column, side, width):
    base = pl.multiple_of(column // LANES * LANES, LANES)
    after = pl.multiple_of(jnp.minimum(base + side, width - LANES), LANES)
    return base, after, column - base


def this_place():
    section = lax.axis_index("depth")
    return section % 2, section // 2


def column_of(places, width, *index):
    return lax.rem(places[index], width)


def window_place(places, home, turn, strip, width, flip=0):
    core, _ = this_place()
    regions = lax.axis_size("scan")
    source = lax.rem(lax.axis_index("scan") - home + regions, regions)
    value = places[core ^ flip, turn]
    return value // width - source * strip, lax.rem(lax.rem(value, width), LANES)


def pick_kernel(waves, out, buffer, arrived):
    core, half = this_place()
    copy = pltpu.make_async_copy(waves.at[core, 1 - half], buffer, arrived)
    copy.start()
    copy.wait()
    out[...] = buffer[...].astype(bf16)


def extract_kernel(reach, *refs):
    places, (strip, *outs) = refs[:reach], refs[reach:]
    count, _, rows, side = outs[0].shape
    width = strip.shape[2]
    core, _ = this_place()
    lane = lax.broadcasted_iota(jnp.int32, (rows, LANES), 1)
    for flip in range(2):
        for step in range(reach):
            out = outs[flip * reach + step]
            for turn in range(count):
                column = column_of(places[step], width, core ^ flip, turn)
                base, after, begin = stretch(column, side, width)
                rest = pl.multiple_of(base + LANES, LANES)
                for plane in range(2):
                    first = strip[plane, :, pl.ds(base, LANES)]
                    again = strip[plane, :, pl.ds(after, LANES)]
                    out[turn, plane, :, :LANES] = jnp.where(lane < begin, again, first).astype(bf16)
                    out[turn, plane, :, LANES:] = strip[plane, :, pl.ds(rest, side - LANES)].astype(
                        bf16
                    )


def start_kernel(home, strip, width, places, probe, *refs):
    adjoints, (left, right, out) = refs[:-3], refs[-3:]
    _, half = this_place()

    @pl.when(half == 0)
    def _():
        for turn in range(len(adjoints)):
            down, across = window_place(places, home, turn, strip, width)
            for plane in range(2):
                out[turn, plane] = turned(probe[plane], down, across)

    @pl.when(half != 0)
    def _():
        fields = []
        for turn, adjoint in enumerate(adjoints):
            down, across = window_place(places, home, turn, strip, width)
            real, imag = (turned(adjoint[plane].astype(f32), down, across) for plane in range(2))
            fields.append((real, -imag))
        for turn, field in enumerate(propagate(fields, left[...], right[...])):
            out[turn, 0], out[turn, 1] = field


def pair(ref, *index):
    return ref[(*index, 0)].astype(f32), ref[(*index, 1)].astype(f32)


def own_first():
    core, half = this_place()
    return jnp.where(core == half, 0, 1)


def near_kernel(home, turn, early, width, places, start, left, right, *refs):
    pieces, (frames, wave, sent) = refs[:-3], refs[-3:]
    reach = len(pieces) // 2
    _, _, strip, side = pieces[0].shape
    own = own_first()
    row = lax.broadcasted_iota(jnp.int32, (strip, side), 0)
    down, _ = window_place(places, home, turn, strip, width)
    for flip in range(2):
        parts = pieces[flip * reach : (flip + 1) * reach]
        for plane in range(2):
            first = parts[0][turn, plane].astype(f32)
            again = parts[-1][turn, plane].astype(f32)
            frames[own ^ flip, plane, :strip] = jnp.where(row < down, again, first).astype(bf16)
            for step in range(1, reach - 1):
                frames[own ^ flip, plane, step * strip : (step + 1) * strip] = parts[step][
                    turn, plane
                ]
    field = multiply(pair(frames, 0), pair(start, turn))
    if early:
        (field,) = propagate([field], left[:, side:], right[side:])
        wave[0], wave[1] = field
        real, imag = multiply(pair(frames, 1), field)
    else:
        (field,) = propagate([field], left[...], right[...])
        wave[0], wave[1] = field
        ((real, imag),) = propagate([multiply(pair(frames, 1), field)], left[...], right[...])
    sent[0] = real.astype(bf16)
    sent[1] = imag.astype(bf16)


def far_kernel(turn, early, start, left, right, frames, wave, arrived, kept, given, last):
    own = own_first()
    side = start.shape[2]
    field = pair(arrived)
    if early:
        (field,) = propagate([field], left[...], right[...])
        outer = multiply(pair(wave), field)
        (field,) = propagate([multiply(pair(frames, 1), field)], left[...], right[...])
    else:
        outer = multiply(pair(wave), field)
        (field,) = propagate([multiply(pair(frames, 1), field)], left[:, side:], right[side:])
    first = multiply(pair(start, turn), field)
    for plane, sign in ((0, 1.0), (1, -1.0)):
        kept[plane] = (jnp.where(own == 0, first[plane], outer[plane]) * sign).astype(bf16)
        given[plane] = (jnp.where(own == 0, outer[plane], first[plane]) * sign).astype(bf16)
    last[0], last[1] = multiply(pair(frames, 0), field)


def part_kernel(home, width, places, *refs):
    count = places.shape[1]
    windows, outs = refs[: 2 * count], refs[2 * count :]
    _, _, _, strip, side = outs[0].shape
    row = lax.broadcasted_iota(jnp.int32, (strip, side), 0)
    for flip in range(2):
        for turn in range(count):
            window = windows[flip * count + turn]
            down, _ = window_place(places, home, turn, strip, width, flip)
            for plane in range(2):
                ends = window[plane, :strip].astype(f32)
                outs[0][flip, turn, plane] = jnp.where(row < down, 0.0, ends).astype(bf16)
                outs[-1][flip, turn, plane] = jnp.where(row < down, ends, 0.0).astype(bf16)
                for step in range(1, len(outs) - 1):
                    outs[step][flip, turn, plane] = window[
                        plane, step * strip : (step + 1) * strip
                    ]


def probe_kernel(home, strip, width, places, *refs):
    waves, (near, away, sent, total) = refs[:-4], refs[-4:]
    core, half = this_place()
    weight = jnp.where(half == 0, 1.0, 0.0)
    for plane, sign in ((0, weight), (1, -weight)):
        parts = []
        for turn, wave in enumerate(waves):
            down, across = window_place(places, home, turn, strip, width)
            parts.append(turned_back(wave[plane], down, across))
        total[plane] = sum(parts) * sign
    height = near.shape[1]
    for index, out in enumerate((near, away)):
        for plane in range(2):
            mine = pl.multiple_of((2 * index + core) * height, height)
            other = pl.multiple_of((2 * index + (core ^ 1)) * height, height)
            out[plane] = total[plane, pl.ds(mine, height)]
            sent[index, plane] = total[plane, pl.ds(other, height)].astype(bf16)


def deposit_kernel(reach, *refs):
    places, pieces, out = refs[:reach], refs[reach:-1], refs[-1]
    _, count, _, strip, side = pieces[0].shape
    width = out.shape[2]
    core, _ = this_place()
    lane = lax.broadcasted_iota(jnp.int32, (strip, LANES), 1)
    out[...] = jnp.zeros(out.shape, f32)
    for step, piece in enumerate(pieces):
        for flip in range(2):
            for turn in range(count):
                column = column_of(places[step], width, core ^ flip, turn)
                base, after, begin = stretch(column, side, width)
                rest = pl.multiple_of(base + LANES, LANES)
                for plane in range(2):
                    ends = piece[flip, turn, plane, :, :LANES].astype(f32)
                    out[plane, :, pl.ds(base, LANES)] += jnp.where(lane < begin, 0.0, ends)
                    out[plane, :, pl.ds(rest, side - LANES)] += piece[
                        flip, turn, plane, :, LANES:
                    ].astype(f32)
                    out[plane, :, pl.ds(after, LANES)] += jnp.where(lane < begin, ends, 0.0)


def local(transmission, probe, exit_adjoint, scan_row, scan_col):
    depth = lax.axis_size("depth")
    regions = lax.axis_size("scan")
    strip, width = transmission.shape[2:]
    side = probe.shape[1]
    reach = side // strip + 1
    home = reach // 2
    count = scan_row.shape[1]
    assert transmission.shape[0] == 1 and depth == 4 and scan_row.shape[0] == 2
    assert side == 2 * LANES and count == 2

    def along_scan(value, by):
        return lax.ppermute(value, "scan", [(i, (i + by) % regions) for i in range(regions)])

    def across(value, flip, by, sections=range(depth)):
        if flip == 0 and by == 0:
            return value
        route = [
            (d * regions + i, (d ^ flip) * regions + (i + by) % regions)
            for d in sections
            for i in range(regions)
        ]
        return lax.ppermute(value, ("depth", "scan"), route)

    smem = pl.BlockSpec(memory_space=pltpu.SMEM)
    vmem = pl.BlockSpec(memory_space=pltpu.VMEM)

    def call(kernel, out_shape, in_specs, flops, name, scratch=(), limit=24):
        return pl.pallas_call(
            kernel,
            out_shape=out_shape,
            in_specs=in_specs,
            out_specs=jax.tree.map(lambda _: vmem, out_shape),
            scratch_shapes=scratch,
            compiler_params=pltpu.CompilerParams(vmem_limit_bytes=limit << 20),
            cost_estimate=pl.CostEstimate(flops=flops, bytes_accessed=4 << 20, transcendentals=0),
            name=name,
        )

    shape = jax.ShapeDtypeStruct
    piece = shape((count, 2, strip, side), bf16)
    wave = (2, side, side)
    field = (count,) + wave
    left, right = (jnp.asarray(table) for table in tables(side))
    lower = range(depth // 2)

    adjoint = call(
        pick_kernel,
        shape(wave, bf16),
        [pl.BlockSpec(memory_space=pltpu.HBM)],
        1 << 20,
        "pick",
        [pltpu.VMEM(wave, f32), pltpu.SemaphoreType.DMA],
        62,
    )(exit_adjoint)
    adjoint, scan_row = lax.optimization_barrier((adjoint, scan_row))
    adjoint = along_scan(adjoint, home)
    packed = scan_row * width + scan_col
    places = [packed] + [along_scan(packed, step) for step in range(1, reach)]

    order = [(flip, step) for flip in range(2) for step in range(reach)]
    far_first = sorted(order, key=lambda key: -abs(key[1] - home))
    pieces = call(
        functools.partial(extract_kernel, reach),
        [piece] * len(order),
        [smem] * reach + [vmem],
        1 << 26,
        "extract",
    )(*places, transmission[0])
    pieces = dict(zip(order, pieces))
    adjoint, pieces[0, home] = lax.optimization_barrier((adjoint, pieces[0, home]))
    adjoints = [adjoint, across(adjoint, 2, 0, lower)]
    for flip, step in far_first:
        if flip == 1 and step in (home, home + 1):
            pieces[flip, step], pieces[0, 0] = lax.optimization_barrier(
                (pieces[flip, step], pieces[0, 0])
            )
        pieces[flip, step] = across(pieces[flip, step], flip, home - step)

    start = call(
        functools.partial(start_kernel, home, strip, width),
        shape(field, f32),
        [smem] + [vmem] * (3 + count),
        1 << 30,
        "start",
    )(places[home], probe, *adjoints, left, right)
    chains = []
    for turn in range(count):
        frames, forward, sent = call(
            functools.partial(near_kernel, home, turn, turn == count - 1, width),
            [shape((2,) + wave, bf16), shape(wave, f32), shape(wave, bf16)],
            [smem] + [vmem] * (3 + len(order)),
            1 << 30,
            "near",
        )(places[home], start, left, right, *(pieces[key] for key in order))
        chains.append((frames, forward, across(sent, 2, 0)))
    kept, given, lasts = [], [], []
    for turn, chain in enumerate(chains):
        mine, other, last = call(
            functools.partial(far_kernel, turn, turn == count - 1),
            [shape(wave, bf16)] * 2 + [shape(wave, f32)],
            [vmem] * 6,
            1 << 31,
            "far",
        )(start, left, right, *chain)
        kept.append(mine)
        given.append(across(other, 1, 0))
        lasts.append(last)
    parts = call(
        functools.partial(part_kernel, home, width),
        [shape((2,) + piece.shape, bf16)] * reach,
        [smem] + [vmem] * (2 * count),
        1 << 26,
        "part",
    )(places[home], *kept, *given)
    parts = list(parts)

    height = side // depth
    near, away, probe_sent = call(
        functools.partial(probe_kernel, home, strip, width),
        [shape((2, height, side), f32)] * 2 + [shape((2, 2, height, side), bf16)],
        [smem] + [vmem] * count,
        1 << 26,
        "probe",
        [pltpu.VMEM(wave, f32)],
    )(places[home], *lasts)
    returned = [across(part, 0, step - home) for step, part in enumerate(parts)]

    def scan_round(total, span):
        rounded = total.astype(bf16)
        route = [(i, i ^ span) for i in range(regions)]
        return rounded.astype(f32) + lax.ppermute(rounded, "scan", route).astype(f32)

    def probe_rounds(_, held):
        near, away, given = held
        away = across((away + given[1].astype(f32)).astype(bf16), 2, 0, lower).astype(f32)
        total = jnp.where(half == 0, near + given[0].astype(f32), away)
        for span in spans[:-1]:
            total = scan_round(total, span)
        return total, away, given

    half = lax.axis_index("depth") // (depth // 2)
    once = lax.axis_index("depth") // depth + 1
    assert regions & (regions - 1) == 0
    spans = [1 << level for level in range(regions.bit_length() - 1)]
    near, parts[home] = lax.optimization_barrier((near, parts[home]))
    probe_grad, *_ = lax.fori_loop(
        0, once, probe_rounds, (near, away, across(probe_sent, 1, 0))
    )
    probe_grad, returned = lax.optimization_barrier((probe_grad, returned))
    probe_grad = scan_round(probe_grad, spans[-1])
    object_grad = call(
        functools.partial(deposit_kernel, reach),
        shape(transmission.shape[1:], f32),
        [smem] * reach + [vmem] * reach,
        1 << 26,
        "deposit",
    )(*places, *returned)
    return object_grad[None], probe_grad


def solution(mesh):
    placed = (
        P("depth", None, "scan", None),
        P(),
        P(None, "scan", None, None, None),
        P(None, "scan"),
        P(None, "scan"),
    )
    return jax.shard_map(
        local,
        mesh=mesh,
        in_specs=placed,
        out_specs=(P("depth", None, "scan", None), P(None, "depth", None)),
        check_vma=False,
    )
```
